512 devices in a mesh: kv: 4 (over z_lo), blk: 128 (over z_hi, x, y, core).
Axes of the slice: x: 4, y: 8, z: 8 (z_hi: 2, z_lo: 4; z = z_hi * 4 + z_lo), core: 2. Of those that a mesh axis runs over, the one named last changes fastest.
Arguments:
- queries: bfloat16 [10240, 2048], P('blk', 'kv'), may hold values from -32 to 32, as said below
- keys: bfloat16 [10240, 512], P('blk', 'kv'), may hold values from -7 to 7, as said below
- values: bfloat16 [10240, 512], P('blk', 'kv'), may hold values from -6 to 6
- lengths: int32 [64], replicated, may hold values from 1 to 80, 2048 in all
- out_weight: bfloat16 [4096, 2048], P('blk', 'kv'), may hold values from -0.125 to 0.125
Outputs:
- hidden: bfloat16 [10240, 4096], P('blk', 'kv')
- cache_keys: bfloat16 [10240, 512], P('blk', 'kv')
The draws below stay inside these ranges and needn't reach their ends.
Inputs may be any that keep to these rules, and one draw needn't show every extreme that they name: `queries`: rotary inputs of order one; in some rows a query head may be a multiple of its key head. `keys`: key projections of order one. `lengths`: each short prompt is 1 to 80 tokens long, one of them exactly 80; their sum is 2048.
All inputs are finite; a program needn't handle non-finite values.
Results may differ from the reference program's by a relative error of at most 0.0095.
Values may be sent and summed in bfloat16 or wider, within the bound.
A program may use at most 64 MiB of HBM per device.

```python
import math
import jax
import jax.numpy as jnp
import numpy as np
from jax import lax

D = 4096
HD = 128
KVH = 4
QPG = 4
TOK_DEV = 80
TOKENS = 10240
LONG = 8192
SHORTS = 64
HQ = 16


def draw_pair(key):
    key_rows = jax.random.normal(jax.random.fold_in(key, 11), (TOKENS, KVH * HD), jnp.float32)
    key_rows = jnp.clip(key_rows, -6.0, 6.0)
    query_rows = 2.0 * jax.random.normal(jax.random.fold_in(key, 12), (TOKENS, KVH * QPG * HD), jnp.float32)
    query_rows = jnp.clip(query_rows, -12.0, 12.0)
    return (query_rows, key_rows)


def draw_queries(key, part):
    return draw_pair(key)[0].astype(jnp.bfloat16)


def draw_keys(key, part):
    return draw_pair(key)[1].astype(jnp.bfloat16)


def levels(rng, dims, cuts, least, high):
    def one(dim, shards_of):
        draws = jax.random.uniform(jax.random.fold_in(jax.random.fold_in(rng, 6), dim), (shards_of,), jnp.float32, least / len(cuts), high / len(cuts))
        return jnp.repeat(jnp.exp(draws), dims[dim] // shards_of).reshape((-1,) + (1,) * (len(dims) - dim - 1))

    factor_of = one(*cuts[0])
    for cut in cuts[1:]:
        factor_of = factor_of * one(*cut)
    return factor_of


def length_profile(count, total, reach, lean):
    loads = [(1 << 20) // math.isqrt(standing ** lean) + 1 for standing in range(2, count + 1)]
    spare, holding = total - reach - (count - 1), [1] * (count - 1)
    while spare > 0:
        candidates = [i for i in range(count - 1) if holding[i] < reach]
        whole, left = sum([loads[i] for i in candidates]), spare
        for i in candidates:
            addition = min(reach - holding[i], max(1, left * loads[i] // whole), spare)
            holding[i] = holding[i] + addition
            spare = spare - addition
    return np.array([reach] + holding)


def ragged_sizes(stream_key, count, total, reach, skew):
    if count == 2:
        one = jax.random.randint(stream_key, (), max(1, total - reach), min(reach, total - 1) + 1)
        return jnp.stack([one, total - one])
    sizes = jnp.asarray(length_profile(count, total, reach, skew), jnp.int32)
    pairs = (count - 1) // 2
    source_of, sink = sizes[1:1 + 2 * pairs:2], sizes[2:2 + 2 * pairs:2]
    room = jnp.minimum(source_of - 1, reach - sink)
    moved = jax.random.randint(jax.random.fold_in(stream_key, 1), (pairs,), 0, 1 << 20) % (room + 1)
    sizes = sizes.at[1:1 + 2 * pairs:2].set(source_of - moved).at[2:2 + 2 * pairs:2].set(sink + moved)
    return sizes[jax.random.permutation(jax.random.fold_in(stream_key, 2), count)]


def normal_values(stream_key, shape, scale, reach, shards=(), dtype=jnp.bfloat16):
    gain = levels(stream_key, shape, shards, -0.22, 0.18) if shards else 1.0
    array = jax.random.normal(stream_key, shape, jnp.float32) * scale * gain
    return jnp.minimum(jnp.maximum(array, -reach), reach).astype(dtype)


def setup_inputs(seed: int = 0) -> dict:
    arg_keys = jax.random.split(jax.random.key(seed), 6)
    queries = draw_queries(jax.random.fold_in(arg_keys[5], 71), 0)
    keys = draw_keys(jax.random.fold_in(arg_keys[5], 71), 0)
    values = normal_values(arg_keys[2], (TOKENS, KVH * HD), 1.0, 6.0, ((0, 128), (1, 4)))
    lengths = ragged_sizes(arg_keys[3], SHORTS, TOKENS - LONG, TOK_DEV, 2).astype(jnp.int32)
    out_weight = normal_values(arg_keys[4], (D, HQ * HD), (HQ * HD) ** -0.5, 0.125, ((0, 128), (1, 4)))
    return {"queries": queries, "keys": keys, "values": values, "lengths": lengths, "out_weight": out_weight}


rope_base = 500000.0


def locate(index, starts):
    hit = starts[None, :] <= index[:, None]
    segment = (jnp.sum(hit.astype(jnp.int32), axis=1) - 1).astype(jnp.int32)
    offset = jnp.max(jnp.where(hit, starts[None, :], 0), axis=1).astype(jnp.int32)
    return segment, offset


def rotate(field, positions):
    half = field.shape[-1] // 2
    steps = jnp.arange(half).astype(jnp.float32) * (2.0 / field.shape[-1])
    inverse = jnp.power(jnp.float32(rope_base), -steps)
    angle = positions.astype(jnp.float32)[:, None, None] * inverse[None, None, :]
    cosine = jnp.cos(angle)
    sine = jnp.sin(angle)
    first = field[..., :half].astype(jnp.float32)
    second = field[..., half:].astype(jnp.float32)
    return jnp.concatenate([first * cosine - second * sine, second * cosine + first * sine], axis=-1)


def reference(queries, keys, values, lengths, out_weight):
    total_len = queries.shape[0]
    long_len = total_len - jnp.sum(lengths)
    shifted = jnp.concatenate([jnp.zeros((1,), jnp.int32), jnp.cumsum(lengths)[:-1].astype(jnp.int32)])
    starts = jnp.concatenate([jnp.zeros((1,), jnp.int32), (long_len + shifted).astype(jnp.int32)])
    index = jnp.arange(total_len).astype(jnp.int32)
    segment, offset = locate(index, starts)
    positions = index - offset
    rot_keys = rotate(keys.reshape(total_len, KVH, HD), positions).astype(jnp.bfloat16)
    rot_queries = rotate(queries.reshape(total_len, HQ, HD), positions).astype(jnp.bfloat16)
    scale = 1.0 / (HD ** 0.5)
    keys_wide = rot_keys.astype(jnp.float32)
    values_wide = values.reshape(total_len, KVH, HD).astype(jnp.float32)
    count = total_len // TOK_DEV

    def attend(block_idx):
        begin = (block_idx * TOK_DEV).astype(jnp.int32)
        query_blk = lax.dynamic_slice_in_dim(rot_queries, begin, TOK_DEV, 0).astype(jnp.float32)
        query_idx = lax.dynamic_slice_in_dim(index, begin, TOK_DEV, 0)
        query_seg = lax.dynamic_slice_in_dim(segment, begin, TOK_DEV, 0)
        live = (segment[None, :] == query_seg[:, None]) & (index[None, :] <= query_idx[:, None])
        pieces = []
        for group in range(KVH):
            group_q = query_blk[:, group * QPG:(group + 1) * QPG]
            scores = jnp.einsum("bhd,nd->bhn", group_q, keys_wide[:, group]) * scale
            scores = jnp.where(live[:, None, :], scores, -1e30)
            row_max = jnp.max(scores, axis=2, keepdims=True)
            expo = jnp.where(live[:, None, :], jnp.exp(scores - row_max), 0.0)
            row_sum = jnp.sum(expo, axis=2, keepdims=True)
            rounded = expo.astype(jnp.bfloat16).astype(jnp.float32)
            weighted = jnp.einsum("bhn,nd->bhd", rounded, values_wide[:, group])
            pieces.append((weighted / row_sum).astype(jnp.bfloat16).reshape(TOK_DEV, QPG * HD))
        return jnp.concatenate(pieces, axis=1)

    attended = lax.map(attend, jnp.arange(count).astype(jnp.int32)).reshape(total_len, HQ * HD)
    width = QPG * HD
    hidden = jnp.zeros((total_len, out_weight.shape[0]), jnp.float32)
    for group in range(KVH):
        part_att = attended[:, group * width:(group + 1) * width]
        part_w = out_weight[:, group * width:(group + 1) * width]
        partial_value = jnp.dot(part_att, part_w.T, preferred_element_type=jnp.float32).astype(jnp.bfloat16)
        partial_value = lax.optimization_barrier(partial_value)
        hidden = hidden + partial_value.astype(jnp.float32)
    return hidden.astype(jnp.bfloat16), rot_keys.reshape(total_len, KVH * HD)
```

```python
import functools

import jax
import jax.numpy as jnp
import numpy as np
from jax import lax
from jax.experimental import pallas as pl
from jax.experimental.pallas import tpu as pltpu
from jax.sharding import PartitionSpec as P

MESH = pl.DeviceIdType.MESH
T, HD, H, NX, NY, G = 80, 128, 4, 4, 8, 4
R = H * T
SUP = 16 * T
CH = NY * T
LONG_BLOCKS = 102
LONG_TOKENS = 8192
TOKENS = 10240
NEG = -1e30
SCALE = float(np.log2(np.e) / np.sqrt(HD))


def dot_nt(a, b):
    return lax.dot_general(a, b, (((1,), (1,)), ((), ())), preferred_element_type=jnp.float32)


def kernel(
    q_ref, k_ref, v_ref, len_ref, w_ref, inv_ref, out_ref, cache_ref,
    kv, qb, acc, mx, sm, osend, ssend, obuf, sbuf, ab, wb, col,
    ys, yr, zs, zr, fs, fr, cs, cr, qs, qr, os_, or_, ss, sr, as_, ar, wds, wdr, wrs, wrr, wcs, wcr, lsem,
):
    blk, g = lax.axis_index("blk"), lax.axis_index("kv")
    c = lax.rem(blk, 2)
    y = lax.rem(lax.div(blk, 2), NY)
    x = lax.rem(lax.div(blk, 16), NX)
    zh = lax.div(blk, 64)
    dest_g = 2 * zh + lax.div(x, 2)
    half = lax.rem(x, 2)

    def at(zh_=zh, x_=x, y_=y, c_=c, g_=g):
        return {"blk": ((zh_ * NX + x_) * NY + y_) * 2 + c_, "kv": g_}

    def send(src, dst, s, r, dev):
        return pltpu.make_async_remote_copy(
            src_ref=src, dst_ref=dst, send_sem=s, recv_sem=r, device_id=dev, device_id_type=MESH
        )

    def yp(d):
        return lax.rem(y + d + NY, NY)

    def xp(d):
        return lax.rem(x + d, NX)

    def gp(d):
        return lax.rem(g + d, G)

    bar = pltpu.get_barrier_semaphore()

    def hello(dev):
        pl.semaphore_signal(bar, inc=1, device_id=dev, device_id_type=MESH)

    hello(at(zh_=1 - zh))
    hello(at(c_=1 - c))
    for d in range(1, NY):
        hello(at(y_=yp(d)))
    for d in range(1, NX):
        hello(at(x_=xp(d)))
    for d in range(1, G):
        hello(at(g_=gp(d)))
    src_zh, src_x = lax.div(g, 2), 2 * lax.rem(g, 2)
    is_src = (src_zh == zh) & (lax.div(x, 2) == lax.rem(g, 2))
    for a in range(2):
        for d in range(G):
            if d == 0:
                @pl.when(jnp.logical_not(is_src & (half == a)))
                def _(a=a):
                    hello(at(zh_=src_zh, x_=src_x + a))
            else:
                hello(at(zh_=src_zh, x_=src_x + a, g_=gp(d)))

    lens = jnp.broadcast_to(len_ref[...].astype(jnp.float32), (8, 64))
    tri = (lax.broadcasted_iota(jnp.int32, (64, 64), 0) < lax.broadcasted_iota(jnp.int32, (64, 64), 1))
    before = jnp.dot(lens, tri.astype(jnp.float32), preferred_element_type=jnp.float32)[:1]
    starts = before + (TOKENS - jnp.sum(lens[:1], axis=1, keepdims=True))

    def first_of(tok):
        return jnp.max(jnp.where(starts <= tok, starts, 0.0), axis=1, keepdims=True)

    row = lax.broadcasted_iota(jnp.int32, (T, 1), 0)
    tok = (row + blk * T).astype(jnp.float32)
    angle = (tok - first_of(tok)) * inv_ref[...]
    cosine = jnp.cos(angle)
    lane = lax.broadcasted_iota(jnp.int32, (T, HD), 1)
    sine = jnp.where(lane < HD // 2, -1.0, 1.0) * jnp.sin(angle)

    def rotate(f):
        f = f.astype(jnp.float32)
        return (f * cosine + pltpu.roll(f, HD // 2, 1) * sine).astype(jnp.bfloat16)

    rk = rotate(k_ref[...])
    cache_ref[...] = rk
    kv[zh, c, y, 0] = rk
    kv[zh, c, y, 1] = v_ref[...]
    for h in range(H):
        qb[x, h * T:(h + 1) * T, :] = rotate(q_ref[:, h * HD:(h + 1) * HD])

    pl.semaphore_wait(bar, 2 + (NY - 1) + (NX - 1) + (G - 1) + 7 + jnp.where(dest_g == g, 0, 1))

    mine = kv.at[zh, c, y]
    zsend = send(mine, mine, zs, zr, at(zh_=1 - zh))

    @pl.when(zh == 0)
    def _():
        zsend.start()

    ysend = [send(mine, mine, ys.at[d - 1], yr.at[d - 1], at(y_=yp(d))) for d in range(1, NY)]
    qsend = [send(qb.at[x], qb.at[x], qs.at[d - 1], qr.at[d - 1], at(x_=xp(d))) for d in range(1, NX)]
    for d in (4, 3, 5, 2, 6, 1, 7):
        ysend[d - 1].start()
    for s in qsend:
        s.start()
    slot = wb.at[y, c, g, half]
    wsend = []
    for dz in range(2):
        for dx in range(NX):
            i = dz * NX + dx
            s = send(w_ref, slot, wds.at[i], wdr.at[half, g], at(zh_=lax.rem(zh + dz, 2), x_=xp(dx), g_=dest_g))
            if i:
                s.start()
            else:
                @pl.when(dest_g != g)
                def _(s=s):
                    s.start()
            wsend.append(s)
    own_w = pltpu.make_async_copy(w_ref, slot, lsem)

    @pl.when(dest_g == g)
    def _():
        own_w.start()

    for i in range(NX):
        tk = (row + ((zh * NX + i) * 16 + 2 * y + c) * T).astype(jnp.float32)
        st = first_of(tk)
        both = jnp.where(lax.broadcasted_iota(jnp.int32, (T, HD), 1) == 0, tk, st)
        for h in range(H):
            col[i, h * T:(h + 1) * T, :] = both
    mx[...] = jnp.full(mx.shape, NEG, jnp.float32)
    sm[...] = jnp.zeros(sm.shape, jnp.float32)
    acc[...] = jnp.zeros(acc.shape, jnp.float32)

    other = kv.at[0, c, y]
    fsend = [send(other, other, fs.at[d - 1], fr.at[d - 1], at(y_=yp(d))) for d in range(1, NY)]

    @pl.when(zh == 1)
    def _():
        zsend.wait_recv()
        for d in (4, 3, 5, 2, 6, 1, 7):
            fsend[d - 1].start()

    def chunk(zk, ck):
        sk = zk * NX + x
        r = lax.broadcasted_iota(jnp.int32, (1, CH), 1)
        key_tok = ((r + lax.div(r, T) * T) + sk * SUP + ck * T).astype(jnp.float32)

        def one(i, _):
            sq = zh * NX + i
            b = sq * 16 + 2 * y + c
            near = (sk == sq) | ((sk == sq - 1) & (2 * y + c == 0))
            live = (sk <= sq) & ((b <= LONG_BLOCKS) | near)
            edge = (sk == sq) | (b >= LONG_BLOCKS)

            def work(masked):
                keys = kv[zk, ck, :, 0].reshape(CH, HD)
                vals = kv[zk, ck, :, 1].reshape(CH, HD)
                s = dot_nt(qb[i], keys) * SCALE
                if masked:
                    ok = (key_tok <= col[i, :, 0:1]) & (key_tok >= col[i, :, 1:2])
                    s = jnp.where(ok, s, NEG)
                old = mx[i, :, 0:1]
                new = jnp.maximum(old, jnp.max(s, axis=1, keepdims=True))
                p = jnp.exp2(s - new)
                if masked:
                    p = jnp.where(ok, p, 0.0)
                keep = jnp.exp2(old - new)
                sm[i] = jnp.broadcast_to(sm[i, :, 0:1] * keep + jnp.sum(p, axis=1, keepdims=True), (R, HD))
                mx[i] = jnp.broadcast_to(new, (R, HD))
                acc[i] = acc[i] * keep + jnp.dot(p.astype(jnp.bfloat16), vals, preferred_element_type=jnp.float32)

            @pl.when(live & edge)
            def _():
                work(True)

            @pl.when(live & jnp.logical_not(edge))
            def _():
                work(False)

            return 0

        lax.fori_loop(0, NX, one, 0)

    def over(zk, i):
        return send(kv.at[zk, c], kv.at[zk, c], cs.at[i], cr.at[i], at(c_=1 - c))

    near_half = over(zh, 0)
    far_half = over(0, 1)
    for s in ysend:
        s.wait_recv()
    near_half.start()
    for s in qsend:
        s.wait_recv()
    chunk(zh, c)

    def ring(sign, step, p):
        i = 0 if sign > 0 else 1
        piece = wb.at[yp(-sign * (step - 1)), c, pl.ds(2 * p, 2)]
        return send(piece, piece, wrs.at[i, step - 1, p], wrr.at[i, step - 1, p], at(y_=yp(sign)))

    def ring_pieces(sign, step):
        return (0, 1) if step < 4 else ((0,) if sign > 0 else (1,))

    def w_over(yy, i):
        return send(wb.at[yy, c], wb.at[yy, c], wcs.at[i], wcr.at[i], at(c_=1 - c))

    all_ring = [(sign, step, p) for step in range(1, 5) for sign in (1, -1) for p in ring_pieces(sign, step)]

    def w_begin():
        for a in range(2):
            for gg in range(G):
                is_own = (gg == g) & (dest_g == g) & (half == a)

                @pl.when(is_own)
                def _():
                    own_w.wait()

                @pl.when(jnp.logical_not(is_own))
                def _(a=a, gg=gg):
                    send(w_ref, wb.at[y, c, gg, a], wds.at[0], wdr.at[a, gg], at(c_=1 - c)).wait_recv()
        for p in range(2):
            for sign in (1, -1):
                ring(sign, 1, p).start()
        w_over(y, 0).start()

    def w_step(step):
        for p in range(2):
            for sign in (1, -1):
                if p in ring_pieces(sign, step):
                    ring(sign, step, p).wait_recv()
                    if step < 4 and p in ring_pieces(sign, step + 1):
                        ring(sign, step + 1, p).start()
        w_over(yp(step), step).start()
        if step < 4:
            w_over(yp(-step), 8 - step).start()

    w_begin()
    near_half.wait_recv()
    chunk(zh, 1 - c)

    @pl.when(zh == 1)
    def _():
        for s in fsend:
            s.wait_recv()
        far_half.start()
        chunk(0, c)
        far_half.wait_recv()
        chunk(0, 1 - c)

    lane_r = lax.broadcasted_iota(jnp.int32, (R, HD), 1)

    def pack(d, _):
        i = lax.rem(x + d, NX)
        osend[i] = acc[i].astype(jnp.bfloat16)
        ssend[i] = jnp.transpose(jnp.where(lane_r == 0, mx[i], sm[i]))[:8]
        return 0

    lax.fori_loop(0, NX, pack, 0)
    ox = [send(osend.at[xp(d)], obuf.at[x], os_.at[d - 1], or_.at[d - 1], at(x_=xp(d))) for d in range(1, NX)]
    sx = [send(ssend.at[xp(d)], sbuf.at[x], ss.at[d - 1], sr.at[d - 1], at(x_=xp(d))) for d in range(1, NX)]
    for s in sx + ox:
        s.start()
    w_step(1)
    for s in sx + ox:
        s.wait_recv()
    stats = [ssend[x]] + [sbuf[xp(d)] for d in range(1, NX)]
    parts = [osend[x]] + [obuf[xp(d)] for d in range(1, NX)]
    top = functools.reduce(jnp.maximum, [s[0:1] for s in stats])
    weight = [jnp.exp2(s[0:1] - top) for s in stats]
    total = sum(s[1:2] * w for s, w in zip(stats, weight))
    att = 0.0
    for o, w in zip(parts, weight):
        att += o.astype(jnp.float32) * jnp.transpose(jnp.broadcast_to(w / total, (HD, R)))
    for h in range(H):
        ab[g, :, h * HD:(h + 1) * HD] = att[h * T:(h + 1) * T].astype(jnp.bfloat16)

    ax = [send(ab.at[g], ab.at[g], as_.at[d - 1], ar.at[d - 1], at(g_=gp(d))) for d in range(1, G)]
    for s in ax:
        s.start()
    for step in (2, 3, 4):
        w_step(step)
    for i in range(NY):
        w_over(yp(i), i).wait_recv()
    for s in ax:
        s.wait_recv()

    for a in range(2):
        total_out = 0.0
        for gg in range(G):
            wmat = wb[:, :, gg, a].reshape(NY * 2 * 32, H * HD)
            total_out += dot_nt(ab[gg], wmat)
        out_ref[:, a * 512:(a + 1) * 512] = total_out.astype(jnp.bfloat16)

    @pl.when(zh == 0)
    def _():
        zsend.wait_send()

    @pl.when(zh == 1)
    def _():
        for s in fsend:
            s.wait_send()
        far_half.wait_send()

    for s in ysend + qsend + [near_half] + wsend[1:] + ox + sx + ax:
        s.wait_send()

    @pl.when(dest_g != g)
    def _():
        wsend[0].wait_send()

    for sign, step, p in all_ring:
        ring(sign, step, p).wait_send()
    for i in range(NY):
        w_over(yp(i), i).wait_send()


def body(queries, keys, values, lengths, out_weight):
    steps = np.arange(HD // 2) * (2.0 / HD)
    inverse = (500000.0 ** -steps).astype(np.float32)
    inverse = jnp.asarray(np.concatenate([inverse, inverse])[None, :])
    vmem = pl.BlockSpec(memory_space=pltpu.VMEM)
    dma = pltpu.SemaphoreType.DMA
    bf, f32 = jnp.bfloat16, jnp.float32
    return pl.pallas_call(
        kernel,
        out_shape=(jax.ShapeDtypeStruct((T, 1024), bf), jax.ShapeDtypeStruct((T, HD), bf)),
        in_specs=[vmem] * 6,
        out_specs=(vmem, vmem),
        scratch_shapes=[
            pltpu.VMEM((2, 2, NY, 2, T, HD), bf),
            pltpu.VMEM((NX, R, HD), bf),
            pltpu.VMEM((NX, R, HD), f32),
            pltpu.VMEM((NX, R, HD), f32),
            pltpu.VMEM((NX, R, HD), f32),
            pltpu.VMEM((NX, R, HD), bf),
            pltpu.VMEM((NX, 8, R), f32),
            pltpu.VMEM((NX, R, HD), bf),
            pltpu.VMEM((NX, 8, R), f32),
            pltpu.VMEM((G, T, H * HD), bf),
            pltpu.VMEM((NY, 2, G, 2, 32, H * HD), bf),
            pltpu.VMEM((NX, R, HD), f32),
            dma((NY - 1,)), dma((NY - 1,)),
            dma, dma,
            dma((NY - 1,)), dma((NY - 1,)),
            dma((2,)), dma((2,)),
            dma((NX - 1,)), dma((NX - 1,)),
            dma((NX - 1,)), dma((NX - 1,)),
            dma((NX - 1,)), dma((NX - 1,)),
            dma((G - 1,)), dma((G - 1,)),
            dma((8,)), dma((2, G)),
            dma((2, 4, 2)), dma((2, 4, 2)),
            dma((NY,)), dma((NY,)),
            dma,
        ],
        compiler_params=pltpu.CompilerParams(
            collective_id=0, has_side_effects=True, vmem_limit_bytes=56 * 2**20
        ),
    )(queries, keys, values, lengths.reshape(1, 64), out_weight, inverse)


def solution(mesh):
    return jax.shard_map(
        body,
        mesh=mesh,
        in_specs=(P("blk", "kv"), P("blk", "kv"), P("blk", "kv"), P(), P("blk", "kv")),
        out_specs=(P("blk", "kv"), P("blk", "kv")),
        check_vma=False,
    )
```

```python
import functools

import jax
import jax.numpy as jnp
import numpy as np
from jax import lax
from jax.experimental import pallas as pl
from jax.experimental.pallas import tpu as pltpu
from jax.sharding import PartitionSpec as P

MESH = pl.DeviceIdType.MESH
T, HD, H, NX, NY, G = 80, 128, 4, 4, 8, 4
R = H * T
SUP = 16 * T
CH = NY * T
LONG_BLOCKS = 102
LONG_TOKENS = 8192
TOKENS = 10240
NEG = -1e30
PLAN = ("WF", "", "RX", "a", "1", "", "2", "b3", "4E")
SCALE = float(np.log2(np.e) / np.sqrt(HD))


def dot_nt(a, b):
    return lax.dot_general(a, b, (((1,), (1,)), ((), ())), preferred_element_type=jnp.float32)


def kernel(
    q_ref, k_ref, v_ref, len_ref, w_ref, inv_ref, out_ref, cache_ref,
    kv, qb, acc, mx, sm, osend, ssend, obuf, sbuf, ab, wa, wb, col,
    ys, yr, zs, zr, fs, fr, cs, cr, qs, qr, os_, or_, ss, sr, as_, ar, wds, wdr, wxs, wxr, wys, wyr, wbs, wbr, wrs, wrr, wcs, wcr, wes, wer, lsem,
):
    blk, g = lax.axis_index("blk"), lax.axis_index("kv")
    c = lax.rem(blk, 2)
    y = lax.rem(lax.div(blk, 2), NY)
    x = lax.rem(lax.div(blk, 16), NX)
    zh = lax.div(blk, 64)
    dest_g = 2 * zh + lax.div(x, 2)
    half = lax.rem(x, 2)

    def at(zh_=zh, x_=x, y_=y, c_=c, g_=g):
        return {"blk": ((zh_ * NX + x_) * NY + y_) * 2 + c_, "kv": g_}

    def send(src, dst, s, r, dev):
        return pltpu.make_async_remote_copy(
            src_ref=src, dst_ref=dst, send_sem=s, recv_sem=r, device_id=dev, device_id_type=MESH
        )

    def yp(d):
        return lax.rem(y + d + NY, NY)

    def xp(d):
        return lax.rem(x + d, NX)

    def gp(d):
        return lax.rem(g + d, G)

    bar = pltpu.get_barrier_semaphore()

    def hello(dev):
        pl.semaphore_signal(bar, inc=1, device_id=dev, device_id_type=MESH)

    hello(at(zh_=1 - zh))
    hello(at(c_=1 - c))
    for d in range(1, NY):
        hello(at(y_=yp(d)))
    for d in range(1, NX):
        hello(at(x_=xp(d)))
    for d in range(1, G):
        hello(at(g_=gp(d)))
    src_zh, src_x = lax.div(g, 2), 2 * lax.rem(g, 2)
    own_w = (x == g) & (dest_g == g)
    for a in range(2):
        @pl.when(jnp.logical_not(own_w & (half == a)))
        def _(a=a):
            hello(at(zh_=src_zh, x_=src_x + a, g_=x))

    lens = jnp.broadcast_to(len_ref[...].astype(jnp.float32), (8, 64))
    tri = (lax.broadcasted_iota(jnp.int32, (64, 64), 0) < lax.broadcasted_iota(jnp.int32, (64, 64), 1))
    before = jnp.dot(lens, tri.astype(jnp.float32), preferred_element_type=jnp.float32)[:1]
    starts = before + (TOKENS - jnp.sum(lens[:1], axis=1, keepdims=True))

    def first_of(tok):
        return jnp.max(jnp.where(starts <= tok, starts, 0.0), axis=1, keepdims=True)

    row = lax.broadcasted_iota(jnp.int32, (T, 1), 0)
    tok = (row + blk * T).astype(jnp.float32)
    angle = (tok - first_of(tok)) * inv_ref[...]
    cosine = jnp.cos(angle)
    lane = lax.broadcasted_iota(jnp.int32, (T, HD), 1)
    sine = jnp.where(lane < HD // 2, -1.0, 1.0) * jnp.sin(angle)

    def rotate(f):
        f = f.astype(jnp.float32)
        return (f * cosine + pltpu.roll(f, HD // 2, 1) * sine).astype(jnp.bfloat16)

    rk = rotate(k_ref[...])
    cache_ref[...] = rk
    kv[zh, c, y, 0] = rk
    kv[zh, c, y, 1] = v_ref[...]
    for h in range(H):
        qb[x, h * T:(h + 1) * T, :] = rotate(q_ref[:, h * HD:(h + 1) * HD])

    pl.semaphore_wait(bar, 2 + (NY - 1) + (NX - 1) + (G - 1) + 2 - jnp.where(own_w, 1, 0))

    mine = kv.at[zh, c, y]
    zsend = send(mine, mine, zs, zr, at(zh_=1 - zh))

    @pl.when(zh == 0)
    def _():
        zsend.start()

    def tree(zk, ss_, rs_):
        me = kv.at[zk, c, y]
        first = [send(me, me, ss_.at[i], rs_.at[i], at(y_=yp(d))) for i, d in enumerate((2, -2, 1, -1))]
        second = []
        for i, sign in enumerate((1, -1)):
            whole = kv.at[zk, c, yp(-2 * sign)]
            part = kv.at[zk, c, yp(-2 * sign), i]
            second.append(send(whole, whole, ss_.at[4 + i], rs_.at[4 + i], at(y_=yp(sign))))
            second.append(send(part, part, ss_.at[6 + i], rs_.at[6 + i], at(y_=yp(2 * sign))))
        return first, second

    near1, near2 = tree(zh, ys, yr)
    far1, far2 = tree(0, fs, fr)
    qsend = [send(qb.at[x], qb.at[x], qs.at[d - 1], qr.at[d - 1], at(x_=xp(d))) for d in range(1, NX)]
    for s in near1 + qsend:
        s.start()

    def first_hop(a, dz):
        slot = wa.at[y, c, g] if a == 0 else wb.at[g, y, c]
        return send(w_ref, slot, wds.at[dz], wdr.at[a], at(zh_=lax.rem(zh + dz, 2), x_=g, g_=dest_g))

    def own_copy(a):
        return pltpu.make_async_copy(w_ref, wa.at[y, c, g] if a == 0 else wb.at[g, y, c], lsem)

    for a in range(2):
        @pl.when(half == a)
        def _(a=a):
            first_hop(a, 1).start()

            @pl.when(own_w)
            def _():
                own_copy(a).start()

            @pl.when(jnp.logical_not(own_w))
            def _():
                first_hop(a, 0).start()

    for i in range(NX):
        tk = (row + ((zh * NX + i) * 16 + 2 * y + c) * T).astype(jnp.float32)
        st = first_of(tk)
        both = jnp.where(lax.broadcasted_iota(jnp.int32, (T, HD), 1) == 0, tk, st)
        for h in range(H):
            col[i, h * T:(h + 1) * T, :] = both
    mx[...] = jnp.full(mx.shape, NEG, jnp.float32)
    sm[...] = jnp.zeros(sm.shape, jnp.float32)
    acc[...] = jnp.zeros(acc.shape, jnp.float32)

    def second(first, then):
        for s in first[:2]:
            s.wait_recv()
        for s in then:
            s.start()

    second(near1, near2)

    @pl.when(zh == 1)
    def _():
        zsend.wait_recv()
        for s in far1:
            s.start()

    def far_second():
        @pl.when(zh == 1)
        def _():
            second(far1, far2)

    wy = [send(wb.at[x, y, c], wb.at[x, y, c], wys.at[d - 1], wyr.at[d - 1], at(y_=yp(d))) for d in range(1, NY)]
    wx = [send(wa.at[y, c, x], wa.at[y, c, x], wxs.at[d - 1], wxr.at[d - 1], at(x_=xp(d))) for d in range(1, NX)]

    def cross_part(i, k):
        return wb.at[i, pl.ds(4 * k, 4), c]

    def cross(d, k):
        part = cross_part(x, k)
        return send(part, part, wbs.at[d - 1, k], wbr.at[d - 1, k], at(x_=xp(d)))

    def ring(sign, step, p):
        i = 0 if sign > 0 else 1
        piece = wa.at[yp(-sign * (step - 1)), c, pl.ds(2 * p, 2)]
        return send(piece, piece, wrs.at[i, step - 1, p], wrr.at[i, step - 1, p], at(y_=yp(sign)))

    def ring_pieces(sign, step):
        return (0, 1) if step < 4 else ((0,) if sign > 0 else (1,))

    def w_over(yy, i):
        return send(wa.at[yy, c], wa.at[yy, c], wcs.at[i], wcr.at[i], at(c_=1 - c))

    def wb_over(d):
        part = wb.at[xp(d), :, c]
        return send(part, part, wes.at[d], wer.at[d], at(c_=1 - c))

    all_ring = [(sign, step, p) for step in range(1, 5) for sign in (1, -1) for p in ring_pieces(sign, step)]

    def w_first():
        for a in range(2):
            here = own_w & (half == a)

            @pl.when(here)
            def _(a=a):
                own_copy(a).wait()

            @pl.when(jnp.logical_not(here))
            def _(a=a):
                first_hop(a, 0).wait_recv()
        for s in wx:
            s.start()
        for d in (4, 3, 5, 2, 6, 1, 7):
            wy[d - 1].start()

    def w_ring_begin():
        for s in wx:
            s.wait_recv()
        for p in range(2):
            for sign in (1, -1):
                ring(sign, 1, p).start()
        w_over(y, 0).start()

    def chunk(zk, ck):
        sk = zk * NX + x
        r = lax.broadcasted_iota(jnp.int32, (1, CH), 1)
        key_tok = ((r + lax.div(r, T) * T) + sk * SUP + ck * T).astype(jnp.float32)

        def one(i, _):
            sq = zh * NX + i
            b = sq * 16 + 2 * y + c
            near = (sk == sq) | ((sk == sq - 1) & (2 * y + c == 0))
            live = (sk <= sq) & ((b <= LONG_BLOCKS) | near)
            edge = (sk == sq) | (b >= LONG_BLOCKS)

            def work(masked):
                keys = kv[zk, ck, :, 0].reshape(CH, HD)
                vals = kv[zk, ck, :, 1].reshape(CH, HD)
                s = dot_nt(qb[i], keys) * SCALE
                if masked:
                    ok = (key_tok <= col[i, :, 0:1]) & (key_tok >= col[i, :, 1:2])
                    s = jnp.where(ok, s, NEG)
                old = mx[i, :, 0:1]
                new = jnp.maximum(old, jnp.max(s, axis=1, keepdims=True))
                p = jnp.exp2(s - new)
                if masked:
                    p = jnp.where(ok, p, 0.0)
                keep = jnp.exp2(old - new)
                sm[i] = jnp.broadcast_to(sm[i, :, 0:1] * keep + jnp.sum(p, axis=1, keepdims=True), (R, HD))
                mx[i] = jnp.broadcast_to(new, (R, HD))
                acc[i] = acc[i] * keep + jnp.dot(p.astype(jnp.bfloat16), vals, preferred_element_type=jnp.float32)

            @pl.when(live & edge)
            def _():
                work(True)

            @pl.when(live & jnp.logical_not(edge))
            def _():
                work(False)

            return 0

        lax.fori_loop(0, NX, one, 0)

    def over(zk, i):
        return send(kv.at[zk, c], kv.at[zk, c], cs.at[i], cr.at[i], at(c_=1 - c))

    def w_cross():
        for s in wy:
            s.wait_recv()
        wb_over(0).start()

    def w_cross_go(k):
        for d in (2, 1, 3):
            cross(d, k).start()

    def w_cross_end():
        for d in range(1, NX):
            for k in range(2):
                cross(d, k).wait_recv()
            wb_over(NX - d).start()

    def w_step(step):
        for p in range(2):
            for sign in (1, -1):
                if p in ring_pieces(sign, step):
                    ring(sign, step, p).wait_recv()
                    if step < 4 and p in ring_pieces(sign, step + 1):
                        ring(sign, step + 1, p).start()
        w_over(yp(step), step).start()
        if step < 4:
            w_over(yp(-step), 8 - step).start()

    work = {
        "W": w_first, "R": w_ring_begin, "X": w_cross, "E": w_cross_end,
        "a": lambda: w_cross_go(0), "b": lambda: w_cross_go(1), "F": far_second,
    }
    for step in range(1, 5):
        work[str(step)] = functools.partial(w_step, step)

    def turn(i):
        for name in PLAN[i]:
            work[name]()

    near_half = over(zh, 0)
    far_half = over(0, 1)
    turn(0)
    for s in near1[2:] + near2:
        s.wait_recv()
    near_half.start()
    for s in qsend:
        s.wait_recv()
    turn(1)

    def stage(i, _):
        @pl.when(i == 1)
        def _():
            turn(2)
            near_half.wait_recv()

        @pl.when(i == 2)
        def _():
            turn(3)

            @pl.when(zh == 1)
            def _():
                for s in far1[2:] + far2:
                    s.wait_recv()
                far_half.start()

            turn(4)

        @pl.when(i == 3)
        def _():
            turn(5)

            @pl.when(zh == 1)
            def _():
                far_half.wait_recv()

        @pl.when((i < 2) | (zh == 1))
        def _():
            chunk(jnp.where(i < 2, zh, 0), jnp.where(lax.rem(i, 2) == 0, c, 1 - c))

        return 0

    lax.fori_loop(0, 4, stage, 0)
    turn(6)

    lane_r = lax.broadcasted_iota(jnp.int32, (R, HD), 1)

    def pack(d, _):
        i = lax.rem(x + d, NX)
        osend[i] = acc[i].astype(jnp.bfloat16)
        ssend[i] = jnp.transpose(jnp.where(lane_r == 0, mx[i], sm[i]))[:8]
        return 0

    lax.fori_loop(0, NX, pack, 0)
    ox = [send(osend.at[xp(d)], obuf.at[x], os_.at[d - 1], or_.at[d - 1], at(x_=xp(d))) for d in range(1, NX)]
    sx = [send(ssend.at[xp(d)], sbuf.at[x], ss.at[d - 1], sr.at[d - 1], at(x_=xp(d))) for d in range(1, NX)]
    for s in sx + ox:
        s.start()
    turn(7)
    for s in sx + ox:
        s.wait_recv()
    stats = [ssend[x]] + [sbuf[xp(d)] for d in range(1, NX)]
    parts = [osend[x]] + [obuf[xp(d)] for d in range(1, NX)]
    top = functools.reduce(jnp.maximum, [s[0:1] for s in stats])
    weight = [jnp.exp2(s[0:1] - top) for s in stats]
    total = sum(s[1:2] * w for s, w in zip(stats, weight))
    att = 0.0
    for o, w in zip(parts, weight):
        att += o.astype(jnp.float32) * jnp.transpose(jnp.broadcast_to(w / total, (HD, R)))
    for h in range(H):
        ab[g, :, h * HD:(h + 1) * HD] = att[h * T:(h + 1) * T].astype(jnp.bfloat16)

    ax = [send(ab.at[g], ab.at[g], as_.at[d - 1], ar.at[d - 1], at(g_=gp(d))) for d in range(1, G)]
    for s in ax:
        s.start()
    turn(8)
    for i in range(NY):
        w_over(yp(i), i).wait_recv()
    for d in range(NX):
        wb_over(d).wait_recv()
    for s in ax:
        s.wait_recv()

    for a in range(2):
        total_out = 0.0
        for gg in range(G):
            wmat = (wa[:, :, gg] if a == 0 else wb[gg]).reshape(NY * 2 * 32, H * HD)
            total_out += dot_nt(ab[gg], wmat)
        out_ref[:, a * 512:(a + 1) * 512] = total_out.astype(jnp.bfloat16)

    @pl.when(zh == 0)
    def _():
        zsend.wait_send()

    @pl.when(zh == 1)
    def _():
        for s in far1 + far2:
            s.wait_send()
        far_half.wait_send()

    for s in near1 + near2 + qsend + [near_half] + wx + wy + [cross(d, k) for d in range(1, NX) for k in range(2)] + ox + sx + ax:
        s.wait_send()
    first_hop(0, 1).wait_send()

    @pl.when(jnp.logical_not(own_w))
    def _():
        first_hop(0, 0).wait_send()

    for sign, step, p in all_ring:
        ring(sign, step, p).wait_send()
    for i in range(NY):
        w_over(yp(i), i).wait_send()
    for d in range(NX):
        wb_over(d).wait_send()


def body(queries, keys, values, lengths, out_weight):
    steps = np.arange(HD // 2) * (2.0 / HD)
    inverse = (500000.0 ** -steps).astype(np.float32)
    inverse = jnp.asarray(np.concatenate([inverse, inverse])[None, :])
    vmem = pl.BlockSpec(memory_space=pltpu.VMEM)
    dma = pltpu.SemaphoreType.DMA
    bf, f32 = jnp.bfloat16, jnp.float32
    return pl.pallas_call(
        kernel,
        out_shape=(jax.ShapeDtypeStruct((T, 1024), bf), jax.ShapeDtypeStruct((T, HD), bf)),
        in_specs=[vmem] * 6,
        out_specs=(vmem, vmem),
        scratch_shapes=[
            pltpu.VMEM((2, 2, NY, 2, T, HD), bf),
            pltpu.VMEM((NX, R, HD), bf),
            pltpu.VMEM((NX, R, HD), f32),
            pltpu.VMEM((NX, R, HD), f32),
            pltpu.VMEM((NX, R, HD), f32),
            pltpu.VMEM((NX, R, HD), bf),
            pltpu.VMEM((NX, 8, R), f32),
            pltpu.VMEM((NX, R, HD), bf),
            pltpu.VMEM((NX, 8, R), f32),
            pltpu.VMEM((G, T, H * HD), bf),
            pltpu.VMEM((NY, 2, G, 32, H * HD), bf),
            pltpu.VMEM((G, NY, 2, 32, H * HD), bf),
            pltpu.VMEM((NX, R, HD), f32),
            dma((8,)), dma((8,)),
            dma, dma,
            dma((8,)), dma((8,)),
            dma((2,)), dma((2,)),
            dma((NX - 1,)), dma((NX - 1,)),
            dma((NX - 1,)), dma((NX - 1,)),
            dma((NX - 1,)), dma((NX - 1,)),
            dma((G - 1,)), dma((G - 1,)),
            dma((2,)), dma((2,)),
            dma((NX - 1,)), dma((NX - 1,)),
            dma((NY - 1,)), dma((NY - 1,)),
            dma((NX - 1, 2)), dma((NX - 1, 2)),
            dma((2, 4, 2)), dma((2, 4, 2)),
            dma((NY,)), dma((NY,)),
            dma((NX,)), dma((NX,)),
            dma,
        ],
        compiler_params=pltpu.CompilerParams(
            collective_id=0, has_side_effects=True, vmem_limit_bytes=56 * 2**20
        ),
    )(queries, keys, values, lengths.reshape(1, 64), out_weight, inverse)


def solution(mesh):
    return jax.shard_map(
        body,
        mesh=mesh,
        in_specs=(P("blk", "kv"), P("blk", "kv"), P("blk", "kv"), P(), P("blk", "kv")),
        out_specs=(P("blk", "kv"), P("blk", "kv")),
        check_vma=False,
    )
```

```python
import functools

import jax
import jax.numpy as jnp
import numpy as np
from jax import lax
from jax.experimental import pallas as pl
from jax.experimental.pallas import tpu as pltpu
from jax.sharding import PartitionSpec as P

MESH = pl.DeviceIdType.MESH
T, HD, H, NX, NY, G = 80, 128, 4, 4, 8, 4
R = H * T
SUP = 16 * T
CH = NY * T
LONG_BLOCKS = 102
LONG_TOKENS = 8192
TOKENS = 10240
NEG = -1e30
PLAN = ("WF", "", "RXa", "", "1", "", "2", "b3", "E4")
SCALE = float(np.log2(np.e) / np.sqrt(HD))


def dot_nt(a, b):
    return lax.dot_general(a, b, (((1,), (1,)), ((), ())), preferred_element_type=jnp.float32)


def kernel(
    q_ref, k_ref, v_ref, len_ref, w_ref, inv_ref, out_ref, cache_ref,
    kv, qb, acc, mx, sm, osend, ssend, obuf, sbuf, ab, wa, wb, col,
    ys, yr, zs, zr, fs, fr, cs, cr, qs, qr, os_, or_, ss, sr, as_, ar, wds, wdr, wxs, wxr, wys, wyr, wbs, wbr, wrs, wrr, wcs, wcr, wes, wer, lsem,
):
    blk, g = lax.axis_index("blk"), lax.axis_index("kv")
    c = lax.rem(blk, 2)
    y = lax.rem(lax.div(blk, 2), NY)
    x = lax.rem(lax.div(blk, 16), NX)
    zh = lax.div(blk, 64)
    dest_g = 2 * zh + lax.div(x, 2)
    half = lax.rem(x, 2)

    def at(zh_=zh, x_=x, y_=y, c_=c, g_=g):
        return {"blk": ((zh_ * NX + x_) * NY + y_) * 2 + c_, "kv": g_}

    def send(src, dst, s, r, dev):
        return pltpu.make_async_remote_copy(
            src_ref=src, dst_ref=dst, send_sem=s, recv_sem=r, device_id=dev, device_id_type=MESH
        )

    def yp(d):
        return lax.rem(y + d + NY, NY)

    def xp(d):
        return lax.rem(x + d, NX)

    def gp(d):
        return lax.rem(g + d, G)

    bar = pltpu.get_barrier_semaphore()

    def hello(dev):
        pl.semaphore_signal(bar, inc=1, device_id=dev, device_id_type=MESH)

    hello(at(zh_=1 - zh))
    hello(at(c_=1 - c))
    for d in range(1, NY):
        hello(at(y_=yp(d)))
    for d in range(1, NX):
        hello(at(x_=xp(d)))
    for d in range(1, G):
        hello(at(g_=gp(d)))
    src_zh, src_x = lax.div(g, 2), 2 * lax.rem(g, 2)
    own_w = (x == g) & (dest_g == g)
    for a in range(2):
        @pl.when(jnp.logical_not(own_w & (half == a)))
        def _(a=a):
            hello(at(zh_=src_zh, x_=src_x + a, g_=x))

    lens = jnp.broadcast_to(len_ref[...].astype(jnp.float32), (8, 64))
    tri = (lax.broadcasted_iota(jnp.int32, (64, 64), 0) < lax.broadcasted_iota(jnp.int32, (64, 64), 1))
    before = jnp.dot(lens, tri.astype(jnp.float32), preferred_element_type=jnp.float32)[:1]
    starts = before + (TOKENS - jnp.sum(lens[:1], axis=1, keepdims=True))

    def first_of(tok):
        return jnp.max(jnp.where(starts <= tok, starts, 0.0), axis=1, keepdims=True)

    row = lax.broadcasted_iota(jnp.int32, (T, 1), 0)
    tok = (row + blk * T).astype(jnp.float32)
    angle = (tok - first_of(tok)) * inv_ref[...]
    cosine = jnp.cos(angle)
    lane = lax.broadcasted_iota(jnp.int32, (T, HD), 1)
    sine = jnp.where(lane < HD // 2, -1.0, 1.0) * jnp.sin(angle)

    def rotate(f):
        f = f.astype(jnp.float32)
        return (f * cosine + pltpu.roll(f, HD // 2, 1) * sine).astype(jnp.bfloat16)

    rk = rotate(k_ref[...])
    cache_ref[...] = rk
    kv[zh, c, y, 0] = rk
    kv[zh, c, y, 1] = v_ref[...]
    for h in range(H):
        qb[x, h * T:(h + 1) * T, :] = rotate(q_ref[:, h * HD:(h + 1) * HD])

    pl.semaphore_wait(bar, 2 + (NY - 1) + (NX - 1) + (G - 1) + 2 - jnp.where(own_w, 1, 0))

    mine = kv.at[zh, c, y]
    zsend = send(mine, mine, zs, zr, at(zh_=1 - zh))

    @pl.when(zh == 0)
    def _():
        zsend.start()

    def tree(zk, ss_, rs_):
        me = kv.at[zk, c, y]
        first = [send(me, me, ss_.at[i], rs_.at[i], at(y_=yp(d))) for i, d in enumerate((2, -2, 1, -1))]
        second = []
        for i, sign in enumerate((1, -1)):
            whole = kv.at[zk, c, yp(-2 * sign)]
            part = kv.at[zk, c, yp(-2 * sign), i]
            second.append(send(whole, whole, ss_.at[4 + i], rs_.at[4 + i], at(y_=yp(sign))))
            second.append(send(part, part, ss_.at[6 + i], rs_.at[6 + i], at(y_=yp(2 * sign))))
        return first, second

    near1, near2 = tree(zh, ys, yr)
    far1, far2 = tree(0, fs, fr)
    qsend = [send(qb.at[x], qb.at[x], qs.at[d - 1], qr.at[d - 1], at(x_=xp(d))) for d in range(1, NX)]
    for s in near1 + qsend:
        s.start()

    def first_hop(a, dz):
        slot = wa.at[y, c, g] if a == 0 else wb.at[g, y, c]
        return send(w_ref, slot, wds.at[dz], wdr.at[a], at(zh_=lax.rem(zh + dz, 2), x_=g, g_=dest_g))

    def own_copy(a):
        return pltpu.make_async_copy(w_ref, wa.at[y, c, g] if a == 0 else wb.at[g, y, c], lsem)

    for a in range(2):
        @pl.when(half == a)
        def _(a=a):
            first_hop(a, 1).start()

            @pl.when(own_w)
            def _():
                own_copy(a).start()

            @pl.when(jnp.logical_not(own_w))
            def _():
                first_hop(a, 0).start()

    for i in range(NX):
        tk = (row + ((zh * NX + i) * 16 + 2 * y + c) * T).astype(jnp.float32)
        st = first_of(tk)
        both = jnp.where(lax.broadcasted_iota(jnp.int32, (T, HD), 1) == 0, tk, st)
        for h in range(H):
            col[i, h * T:(h + 1) * T, :] = both
    mx[...] = jnp.full(mx.shape, NEG, jnp.float32)
    sm[...] = jnp.zeros(sm.shape, jnp.float32)
    acc[...] = jnp.zeros(acc.shape, jnp.float32)

    def second(first, then):
        for s in first[:2]:
            s.wait_recv()
        for s in then:
            s.start()

    second(near1, near2)

    @pl.when(zh == 1)
    def _():
        zsend.wait_recv()
        for s in far1:
            s.start()

    def far_second():
        @pl.when(zh == 1)
        def _():
            second(far1, far2)

    wy = [send(wb.at[x, y, c], wb.at[x, y, c], wys.at[d - 1], wyr.at[d - 1], at(y_=yp(d))) for d in range(1, NY)]
    wx = [send(wa.at[y, c, x], wa.at[y, c, x], wxs.at[d - 1], wxr.at[d - 1], at(x_=xp(d))) for d in range(1, NX)]

    whole_x = wb.at[x, :, c]
    cross1 = [send(whole_x, whole_x, wbs.at[i], wbr.at[i], at(x_=xp(d))) for i, d in enumerate((1, NX - 1))]
    cross2 = []
    for i, d in enumerate((1, NX - 1)):
        part = wb.at[xp(NX - d), pl.ds(4 * i, 4), c]
        cross2.append(send(part, part, wbs.at[2 + i], wbr.at[2 + i], at(x_=xp(d))))

    def ring(sign, step, p):
        i = 0 if sign > 0 else 1
        piece = wa.at[yp(-sign * (step - 1)), c, pl.ds(2 * p, 2)]
        return send(piece, piece, wrs.at[i, step - 1, p], wrr.at[i, step - 1, p], at(y_=yp(sign)))

    def ring_pieces(sign, step):
        return (0, 1) if step < 4 else ((0,) if sign > 0 else (1,))

    def w_over(yy, i):
        return send(wa.at[yy, c], wa.at[yy, c], wcs.at[i], wcr.at[i], at(c_=1 - c))

    def wb_over(d):
        part = wb.at[xp(d), :, c]
        return send(part, part, wes.at[d], wer.at[d], at(c_=1 - c))

    all_ring = [(sign, step, p) for step in range(1, 5) for sign in (1, -1) for p in ring_pieces(sign, step)]

    def w_first():
        for a in range(2):
            here = own_w & (half == a)

            @pl.when(here)
            def _(a=a):
                own_copy(a).wait()

            @pl.when(jnp.logical_not(here))
            def _(a=a):
                first_hop(a, 0).wait_recv()
        for s in wx:
            s.start()
        for d in (4, 3, 5, 2, 6, 1, 7):
            wy[d - 1].start()

    def w_ring_begin():
        for s in wx:
            s.wait_recv()
        for p in range(2):
            for sign in (1, -1):
                ring(sign, 1, p).start()
        w_over(y, 0).start()

    def chunk(zk, ck):
        sk = zk * NX + x
        r = lax.broadcasted_iota(jnp.int32, (1, CH), 1)
        key_tok = ((r + lax.div(r, T) * T) + sk * SUP + ck * T).astype(jnp.float32)

        def one(i, _):
            sq = zh * NX + i
            b = sq * 16 + 2 * y + c
            near = (sk == sq) | ((sk == sq - 1) & (2 * y + c == 0))
            live = (sk <= sq) & ((b <= LONG_BLOCKS) | near)
            edge = (sk == sq) | (b >= LONG_BLOCKS)

            def work(masked):
                keys = kv[zk, ck, :, 0].reshape(CH, HD)
                vals = kv[zk, ck, :, 1].reshape(CH, HD)
                s = dot_nt(qb[i], keys) * SCALE
                if masked:
                    ok = (key_tok <= col[i, :, 0:1]) & (key_tok >= col[i, :, 1:2])
                    s = jnp.where(ok, s, NEG)
                old = mx[i, :, 0:1]
                new = jnp.maximum(old, jnp.max(s, axis=1, keepdims=True))
                p = jnp.exp2(s - new)
                if masked:
                    p = jnp.where(ok, p, 0.0)
                keep = jnp.exp2(old - new)
                sm[i] = jnp.broadcast_to(sm[i, :, 0:1] * keep + jnp.sum(p, axis=1, keepdims=True), (R, HD))
                mx[i] = jnp.broadcast_to(new, (R, HD))
                acc[i] = acc[i] * keep + jnp.dot(p.astype(jnp.bfloat16), vals, preferred_element_type=jnp.float32)

            @pl.when(live & edge)
            def _():
                work(True)

            @pl.when(live & jnp.logical_not(edge))
            def _():
                work(False)

            return 0

        lax.fori_loop(0, NX, one, 0)

    def over(zk, i):
        return send(kv.at[zk, c], kv.at[zk, c], cs.at[i], cr.at[i], at(c_=1 - c))

    def w_cross():
        for s in wy:
            s.wait_recv()
        wb_over(0).start()

    def w_cross_one():
        for s in cross1:
            s.start()

    def w_cross_two():
        for s in cross1:
            s.wait_recv()
        for s in cross2:
            s.start()
        wb_over(1).start()
        wb_over(NX - 1).start()

    def w_cross_end():
        for s in cross2:
            s.wait_recv()
        wb_over(2).start()

    def w_step(step):
        for p in range(2):
            for sign in (1, -1):
                if p in ring_pieces(sign, step):
                    ring(sign, step, p).wait_recv()
                    if step < 4 and p in ring_pieces(sign, step + 1):
                        ring(sign, step + 1, p).start()
        w_over(yp(step), step).start()
        if step < 4:
            w_over(yp(-step), 8 - step).start()

    work = {
        "W": w_first, "R": w_ring_begin, "X": w_cross, "E": w_cross_end,
        "a": w_cross_one, "b": w_cross_two, "F": far_second,
    }
    for step in range(1, 5):
        work[str(step)] = functools.partial(w_step, step)

    def turn(i):
        for name in PLAN[i]:
            work[name]()

    near_half = over(zh, 0)
    far_half = over(0, 1)
    turn(0)
    for s in near1[2:] + near2:
        s.wait_recv()
    near_half.start()
    for s in qsend:
        s.wait_recv()
    turn(1)

    def stage(i, _):
        @pl.when(i == 1)
        def _():
            turn(2)
            near_half.wait_recv()

        @pl.when(i == 2)
        def _():
            turn(3)

            @pl.when(zh == 1)
            def _():
                for s in far1[2:] + far2:
                    s.wait_recv()
                far_half.start()

            turn(4)

        @pl.when(i == 3)
        def _():
            turn(5)

            @pl.when(zh == 1)
            def _():
                far_half.wait_recv()

        @pl.when((i < 2) | (zh == 1))
        def _():
            chunk(jnp.where(i < 2, zh, 0), jnp.where(lax.rem(i, 2) == 0, c, 1 - c))

        return 0

    lax.fori_loop(0, 4, stage, 0)
    turn(6)

    lane_r = lax.broadcasted_iota(jnp.int32, (R, HD), 1)

    def pack(i):
        osend[i] = acc[i].astype(jnp.bfloat16)
        ssend[i] = jnp.transpose(jnp.where(lane_r == 0, mx[i], sm[i]))[:8]

    ox = [send(osend.at[xp(d)], obuf.at[x], os_.at[d - 1], or_.at[d - 1], at(x_=xp(d))) for d in range(1, NX)]
    sx = [send(ssend.at[xp(d)], sbuf.at[x], ss.at[d - 1], sr.at[d - 1], at(x_=xp(d))) for d in range(1, NX)]
    for d in (2, 1, 3, 0):
        pack(xp(d))
        if d:
            ox[d - 1].start()
            sx[d - 1].start()
    turn(7)
    for s in sx + ox:
        s.wait_recv()
    stats = [ssend[x]] + [sbuf[xp(d)] for d in range(1, NX)]
    parts = [osend[x]] + [obuf[xp(d)] for d in range(1, NX)]
    top = functools.reduce(jnp.maximum, [s[0:1] for s in stats])
    weight = [jnp.exp2(s[0:1] - top) for s in stats]
    total = sum(s[1:2] * w for s, w in zip(stats, weight))
    att = 0.0
    for o, w in zip(parts, weight):
        att += o.astype(jnp.float32) * jnp.transpose(jnp.broadcast_to(w / total, (HD, R)))
    for h in range(H):
        ab[g, :, h * HD:(h + 1) * HD] = att[h * T:(h + 1) * T].astype(jnp.bfloat16)

    ax = [send(ab.at[g], ab.at[g], as_.at[d - 1], ar.at[d - 1], at(g_=gp(d))) for d in range(1, G)]
    for s in ax:
        s.start()
    turn(8)
    for i in range(NY):
        w_over(yp(i), i).wait_recv()
    for d in range(NX):
        wb_over(d).wait_recv()

    total_out = [0.0, 0.0]
    for d in range(G):
        gg = gp(d)
        if d:
            ax[G - d - 1].wait_recv()
        for a in range(2):
            wmat = (wa[:, :, gg] if a == 0 else wb[gg]).reshape(NY * 2 * 32, H * HD)
            total_out[a] += dot_nt(ab[gg], wmat)
    for a in range(2):
        out_ref[:, a * 512:(a + 1) * 512] = total_out[a].astype(jnp.bfloat16)

    @pl.when(zh == 0)
    def _():
        zsend.wait_send()

    @pl.when(zh == 1)
    def _():
        for s in far1 + far2:
            s.wait_send()
        far_half.wait_send()

    for s in near1 + near2 + qsend + [near_half] + wx + wy + cross1 + cross2 + ox + sx + ax:
        s.wait_send()
    first_hop(0, 1).wait_send()

    @pl.when(jnp.logical_not(own_w))
    def _():
        first_hop(0, 0).wait_send()

    for sign, step, p in all_ring:
        ring(sign, step, p).wait_send()
    for i in range(NY):
        w_over(yp(i), i).wait_send()
    for d in range(NX):
        wb_over(d).wait_send()


def body(queries, keys, values, lengths, out_weight):
    steps = np.arange(HD // 2) * (2.0 / HD)
    inverse = (500000.0 ** -steps).astype(np.float32)
    inverse = jnp.asarray(np.concatenate([inverse, inverse])[None, :])
    vmem = pl.BlockSpec(memory_space=pltpu.VMEM)
    dma = pltpu.SemaphoreType.DMA
    bf, f32 = jnp.bfloat16, jnp.float32
    return pl.pallas_call(
        kernel,
        out_shape=(jax.ShapeDtypeStruct((T, 1024), bf), jax.ShapeDtypeStruct((T, HD), bf)),
        in_specs=[vmem] * 6,
        out_specs=(vmem, vmem),
        scratch_shapes=[
            pltpu.VMEM((2, 2, NY, 2, T, HD), bf),
            pltpu.VMEM((NX, R, HD), bf),
            pltpu.VMEM((NX, R, HD), f32),
            pltpu.VMEM((NX, R, HD), f32),
            pltpu.VMEM((NX, R, HD), f32),
            pltpu.VMEM((NX, R, HD), bf),
            pltpu.VMEM((NX, 8, R), f32),
            pltpu.VMEM((NX, R, HD), bf),
            pltpu.VMEM((NX, 8, R), f32),
            pltpu.VMEM((G, T, H * HD), bf),
            pltpu.VMEM((NY, 2, G, 32, H * HD), bf),
            pltpu.VMEM((G, NY, 2, 32, H * HD), bf),
            pltpu.VMEM((NX, R, HD), f32),
            dma((8,)), dma((8,)),
            dma, dma,
            dma((8,)), dma((8,)),
            dma((2,)), dma((2,)),
            dma((NX - 1,)), dma((NX - 1,)),
            dma((NX - 1,)), dma((NX - 1,)),
            dma((NX - 1,)), dma((NX - 1,)),
            dma((G - 1,)), dma((G - 1,)),
            dma((2,)), dma((2,)),
            dma((NX - 1,)), dma((NX - 1,)),
            dma((NY - 1,)), dma((NY - 1,)),
            dma((4,)), dma((4,)),
            dma((2, 4, 2)), dma((2, 4, 2)),
            dma((NY,)), dma((NY,)),
            dma((NX,)), dma((NX,)),
            dma,
        ],
        compiler_params=pltpu.CompilerParams(
            collective_id=0, has_side_effects=True, vmem_limit_bytes=56 * 2**20
        ),
    )(queries, keys, values, lengths.reshape(1, 64), out_weight, inverse)


def solution(mesh):
    return jax.shard_map(
        body,
        mesh=mesh,
        in_specs=(P("blk", "kv"), P("blk", "kv"), P("blk", "kv"), P(), P("blk", "kv")),
        out_specs=(P("blk", "kv"), P("blk", "kv")),
        check_vma=False,
    )
```

```python
import functools

import jax
import jax.numpy as jnp
import numpy as np
from jax import lax
from jax.experimental import pallas as pl
from jax.experimental.pallas import tpu as pltpu
from jax.sharding import PartitionSpec as P

MESH = pl.DeviceIdType.MESH
T, HD, H, NX, NY, G = 80, 128, 4, 4, 8, 4
R = H * T
SUP = 16 * T
CH = NY * T
LONG_BLOCKS = 102
LONG_TOKENS = 8192
TOKENS = 10240
NEG = -1e30
PLAN = ("WFT", "R", "Xa", "", "1", "", "2", "b3", "E4")
SCALE = float(np.log2(np.e) / np.sqrt(HD))


def dot_nt(a, b):
    return lax.dot_general(a, b, (((1,), (1,)), ((), ())), preferred_element_type=jnp.float32)


def kernel(
    q_ref, k_ref, v_ref, len_ref, w_ref, inv_ref, out_ref, cache_ref,
    kv, qb, acc, mx, sm, osend, ssend, obuf, sbuf, ab, wa, wb, col,
    ys, yr, zs, zr, fs, fr, cs, cr, qs, qr, os_, or_, ss, sr, as_, ar, wds, wdr, wxs, wxr, wys, wyr, wbs, wbr, wrs, wrr, wcs, wcr, wes, wer, lsem,
):
    blk, g = lax.axis_index("blk"), lax.axis_index("kv")
    c = lax.rem(blk, 2)
    y = lax.rem(lax.div(blk, 2), NY)
    x = lax.rem(lax.div(blk, 16), NX)
    zh = lax.div(blk, 64)
    dest_g = 2 * zh + lax.div(x, 2)
    half = lax.rem(x, 2)

    def at(zh_=zh, x_=x, y_=y, c_=c, g_=g):
        return {"blk": ((zh_ * NX + x_) * NY + y_) * 2 + c_, "kv": g_}

    def send(src, dst, s, r, dev):
        return pltpu.make_async_remote_copy(
            src_ref=src, dst_ref=dst, send_sem=s, recv_sem=r, device_id=dev, device_id_type=MESH
        )

    def yp(d):
        return lax.rem(y + d + NY, NY)

    def xp(d):
        return lax.rem(x + d, NX)

    def gp(d):
        return lax.rem(g + d, G)

    bar = pltpu.get_barrier_semaphore()

    def hello(dev):
        pl.semaphore_signal(bar, inc=1, device_id=dev, device_id_type=MESH)

    hello(at(zh_=1 - zh))
    hello(at(c_=1 - c))
    for d in range(1, NY):
        hello(at(y_=yp(d)))
    for d in range(1, NX):
        hello(at(x_=xp(d)))
    for d in range(1, G):
        hello(at(g_=gp(d)))
    src_zh, src_x = lax.div(g, 2), 2 * lax.rem(g, 2)
    own_w = (x == g) & (dest_g == g)
    for a in range(2):
        @pl.when(jnp.logical_not(own_w & (half == a)))
        def _(a=a):
            hello(at(zh_=src_zh, x_=src_x + a, g_=x))

    lens = jnp.broadcast_to(len_ref[...].astype(jnp.float32), (8, 64))
    tri = (lax.broadcasted_iota(jnp.int32, (64, 64), 0) < lax.broadcasted_iota(jnp.int32, (64, 64), 1))
    before = jnp.dot(lens, tri.astype(jnp.float32), preferred_element_type=jnp.float32)[:1]
    starts = before + (TOKENS - jnp.sum(lens[:1], axis=1, keepdims=True))

    def first_of(tok):
        return jnp.max(jnp.where(starts <= tok, starts, 0.0), axis=1, keepdims=True)

    row = lax.broadcasted_iota(jnp.int32, (T, 1), 0)
    tok = (row + blk * T).astype(jnp.float32)
    angle = (tok - first_of(tok)) * inv_ref[...]
    cosine = jnp.cos(angle)
    lane = lax.broadcasted_iota(jnp.int32, (T, HD), 1)
    sine = jnp.where(lane < HD // 2, -1.0, 1.0) * jnp.sin(angle)

    def rotate(f):
        f = f.astype(jnp.float32)
        return (f * cosine + pltpu.roll(f, HD // 2, 1) * sine).astype(jnp.bfloat16)

    rk = rotate(k_ref[...])
    cache_ref[...] = rk
    kv[zh, c, y, 0] = rk
    kv[zh, c, y, 1] = v_ref[...]
    for h in range(H):
        qb[x, h * T:(h + 1) * T, :] = rotate(q_ref[:, h * HD:(h + 1) * HD])

    pl.semaphore_wait(bar, 2 + (NY - 1) + (NX - 1) + (G - 1) + 2 - jnp.where(own_w, 1, 0))

    mine = kv.at[zh, c, y]
    zsend = send(mine, mine, zs, zr, at(zh_=1 - zh))

    @pl.when(zh == 0)
    def _():
        zsend.start()

    def tree(zk, ss_, rs_):
        me = kv.at[zk, c, y]
        first = [send(me, me, ss_.at[i], rs_.at[i], at(y_=yp(d))) for i, d in enumerate((2, -2, 1, -1))]
        second = []
        for i, sign in enumerate((1, -1)):
            whole = kv.at[zk, c, yp(-2 * sign)]
            part = kv.at[zk, c, yp(-2 * sign), i]
            second.append(send(whole, whole, ss_.at[4 + i], rs_.at[4 + i], at(y_=yp(sign))))
            second.append(send(part, part, ss_.at[6 + i], rs_.at[6 + i], at(y_=yp(2 * sign))))
        return first, second

    near1, near2 = tree(zh, ys, yr)
    far1, far2 = tree(0, fs, fr)
    qsend = [send(qb.at[x], qb.at[x], qs.at[d - 1], qr.at[d - 1], at(x_=xp(d))) for d in range(1, NX)]
    for s in near1 + qsend:
        s.start()

    def first_hop(a, dz):
        slot = wa.at[y, c, g] if a == 0 else wb.at[g, y, c]
        return send(w_ref, slot, wds.at[dz], wdr.at[a], at(zh_=lax.rem(zh + dz, 2), x_=g, g_=dest_g))

    def own_copy(a):
        return pltpu.make_async_copy(w_ref, wa.at[y, c, g] if a == 0 else wb.at[g, y, c], lsem)

    for a in range(2):
        @pl.when(half == a)
        def _(a=a):
            first_hop(a, 1).start()

            @pl.when(own_w)
            def _():
                own_copy(a).start()

            @pl.when(jnp.logical_not(own_w))
            def _():
                first_hop(a, 0).start()

    for i in range(NX):
        tk = (row + ((zh * NX + i) * 16 + 2 * y + c) * T).astype(jnp.float32)
        st = first_of(tk)
        both = jnp.where(lax.broadcasted_iota(jnp.int32, (T, HD), 1) == 0, tk, st)
        for h in range(H):
            col[i, h * T:(h + 1) * T, :] = both
    mx[...] = jnp.full(mx.shape, NEG, jnp.float32)
    sm[...] = jnp.zeros(sm.shape, jnp.float32)
    acc[...] = jnp.zeros(acc.shape, jnp.float32)

    def second(first, then):
        for s in first[:2]:
            s.wait_recv()
        for s in then:
            s.start()

    second(near1, near2)

    @pl.when(zh == 1)
    def _():
        zsend.wait_recv()
        for s in far1:
            s.start()

    def far_second():
        @pl.when(zh == 1)
        def _():
            second(far1, far2)

    whole_y = wb.at[x, y, c]
    wy1 = [send(whole_y, whole_y, wys.at[i], wyr.at[i], at(y_=yp(d))) for i, d in enumerate((2, -2, 1, -1))]
    wy2 = []
    for i, sign in enumerate((1, -1)):
        full = wb.at[x, yp(-2 * sign), c]
        part = wb.at[x, yp(-2 * sign), c, pl.ds(16 * i, 16)]
        wy2.append(send(full, full, wys.at[4 + i], wyr.at[4 + i], at(y_=yp(sign))))
        wy2.append(send(part, part, wys.at[6 + i], wyr.at[6 + i], at(y_=yp(2 * sign))))
    wx = [send(wa.at[y, c, x], wa.at[y, c, x], wxs.at[d - 1], wxr.at[d - 1], at(x_=xp(d))) for d in range(1, NX)]

    whole_x = wb.at[x, :, c]
    cross1 = [send(whole_x, whole_x, wbs.at[i], wbr.at[i], at(x_=xp(d))) for i, d in enumerate((1, NX - 1))]
    cross2 = []
    for i, d in enumerate((1, NX - 1)):
        part = wb.at[xp(NX - d), pl.ds(4 * i, 4), c]
        cross2.append(send(part, part, wbs.at[2 + i], wbr.at[2 + i], at(x_=xp(d))))

    def ring(sign, step, p):
        i = 0 if sign > 0 else 1
        piece = wa.at[yp(-sign * (step - 1)), c, pl.ds(2 * p, 2)]
        return send(piece, piece, wrs.at[i, step - 1, p], wrr.at[i, step - 1, p], at(y_=yp(sign)))

    def ring_pieces(sign, step):
        return (0, 1) if step < 4 else ((0,) if sign > 0 else (1,))

    def w_over(yy, i):
        return send(wa.at[yy, c], wa.at[yy, c], wcs.at[i], wcr.at[i], at(c_=1 - c))

    def wb_over(d):
        part = wb.at[xp(d), :, c]
        return send(part, part, wes.at[d], wer.at[d], at(c_=1 - c))

    all_ring = [(sign, step, p) for step in range(1, 5) for sign in (1, -1) for p in ring_pieces(sign, step)]

    def w_first():
        for a in range(2):
            here = own_w & (half == a)

            @pl.when(here)
            def _(a=a):
                own_copy(a).wait()

            @pl.when(jnp.logical_not(here))
            def _(a=a):
                first_hop(a, 0).wait_recv()
        for s in wx:
            s.start()
        for s in wy1:
            s.start()

    def w_ring_begin():
        for s in wx:
            s.wait_recv()
        for p in range(2):
            for sign in (1, -1):
                ring(sign, 1, p).start()
        w_over(y, 0).start()

    def chunk(zk, ck):
        sk = zk * NX + x
        r = lax.broadcasted_iota(jnp.int32, (1, CH), 1)
        key_tok = ((r + lax.div(r, T) * T) + sk * SUP + ck * T).astype(jnp.float32)

        def one(i, _):
            sq = zh * NX + i
            b = sq * 16 + 2 * y + c
            near = (sk == sq) | ((sk == sq - 1) & (2 * y + c == 0))
            live = (sk <= sq) & ((b <= LONG_BLOCKS) | near)
            edge = (sk == sq) | (b >= LONG_BLOCKS)

            def work(masked):
                keys = kv[zk, ck, :, 0].reshape(CH, HD)
                vals = kv[zk, ck, :, 1].reshape(CH, HD)
                s = dot_nt(qb[i], keys) * SCALE
                if masked:
                    ok = (key_tok <= col[i, :, 0:1]) & (key_tok >= col[i, :, 1:2])
                    s = jnp.where(ok, s, NEG)
                old = mx[i, :, 0:1]
                new = jnp.maximum(old, jnp.max(s, axis=1, keepdims=True))
                p = jnp.exp2(s - new)
                if masked:
                    p = jnp.where(ok, p, 0.0)
                keep = jnp.exp2(old - new)
                sm[i] = jnp.broadcast_to(sm[i, :, 0:1] * keep + jnp.sum(p, axis=1, keepdims=True), (R, HD))
                mx[i] = jnp.broadcast_to(new, (R, HD))
                acc[i] = acc[i] * keep + jnp.dot(p.astype(jnp.bfloat16), vals, preferred_element_type=jnp.float32)

            @pl.when(live & edge)
            def _():
                work(True)

            @pl.when(live & jnp.logical_not(edge))
            def _():
                work(False)

            return 0

        lax.fori_loop(0, NX, one, 0)

    def over(zk, i):
        return send(kv.at[zk, c], kv.at[zk, c], cs.at[i], cr.at[i], at(c_=1 - c))

    def w_cross():
        for s in wy1[2:] + wy2:
            s.wait_recv()
        wb_over(0).start()

    def w_cross_one():
        for s in cross1:
            s.start()

    def w_cross_two():
        for s in cross1:
            s.wait_recv()
        for s in cross2:
            s.start()
        wb_over(1).start()
        wb_over(NX - 1).start()

    def w_cross_end():
        for s in cross2:
            s.wait_recv()
        wb_over(2).start()

    def w_step(step):
        for p in range(2):
            for sign in (1, -1):
                if p in ring_pieces(sign, step):
                    ring(sign, step, p).wait_recv()
                    if step < 4 and p in ring_pieces(sign, step + 1):
                        ring(sign, step + 1, p).start()
        w_over(yp(step), step).start()
        if step < 4:
            w_over(yp(-step), 8 - step).start()

    work = {
        "W": w_first, "R": w_ring_begin, "X": w_cross, "E": w_cross_end,
        "a": w_cross_one, "b": w_cross_two, "F": far_second, "T": lambda: second(wy1, wy2),
    }
    for step in range(1, 5):
        work[str(step)] = functools.partial(w_step, step)

    def turn(i):
        for name in PLAN[i]:
            work[name]()

    near_half = over(zh, 0)
    far_half = over(0, 1)
    turn(0)
    for s in near1[2:] + near2:
        s.wait_recv()
    near_half.start()
    for s in qsend:
        s.wait_recv()
    turn(1)

    def stage(i, _):
        @pl.when(i == 1)
        def _():
            turn(2)
            near_half.wait_recv()

        @pl.when(i == 2)
        def _():
            turn(3)

            @pl.when(zh == 1)
            def _():
                for s in far1[2:] + far2:
                    s.wait_recv()
                far_half.start()

            turn(4)

        @pl.when(i == 3)
        def _():
            turn(5)

            @pl.when(zh == 1)
            def _():
                far_half.wait_recv()

        @pl.when((i < 2) | (zh == 1))
        def _():
            chunk(jnp.where(i < 2, zh, 0), jnp.where(lax.rem(i, 2) == 0, c, 1 - c))

        return 0

    lax.fori_loop(0, 4, stage, 0)
    turn(6)

    lane_r = lax.broadcasted_iota(jnp.int32, (R, HD), 1)

    def pack(i):
        osend[i] = acc[i].astype(jnp.bfloat16)
        ssend[i] = jnp.transpose(jnp.where(lane_r == 0, mx[i], sm[i]))[:8]

    ox = [send(osend.at[xp(d)], obuf.at[x], os_.at[d - 1], or_.at[d - 1], at(x_=xp(d))) for d in range(1, NX)]
    sx = [send(ssend.at[xp(d)], sbuf.at[x], ss.at[d - 1], sr.at[d - 1], at(x_=xp(d))) for d in range(1, NX)]
    for d in (2, 1, 3, 0):
        pack(xp(d))
        if d:
            ox[d - 1].start()
            sx[d - 1].start()
    turn(7)
    for s in sx + ox:
        s.wait_recv()
    stats = [ssend[x]] + [sbuf[xp(d)] for d in range(1, NX)]
    parts = [osend[x]] + [obuf[xp(d)] for d in range(1, NX)]
    top = functools.reduce(jnp.maximum, [s[0:1] for s in stats])
    weight = [jnp.exp2(s[0:1] - top) for s in stats]
    total = sum(s[1:2] * w for s, w in zip(stats, weight))
    att = 0.0
    for o, w in zip(parts, weight):
        att += o.astype(jnp.float32) * jnp.transpose(jnp.broadcast_to(w / total, (HD, R)))
    for h in range(H):
        ab[g, :, h * HD:(h + 1) * HD] = att[h * T:(h + 1) * T].astype(jnp.bfloat16)

    ax = [send(ab.at[g], ab.at[g], as_.at[d - 1], ar.at[d - 1], at(g_=gp(d))) for d in range(1, G)]
    for s in ax:
        s.start()
    turn(8)
    for i in range(NY):
        w_over(yp(i), i).wait_recv()
    for d in range(NX):
        wb_over(d).wait_recv()

    total_out = [0.0, 0.0]
    for d in range(G):
        gg = gp(d)
        if d:
            ax[G - d - 1].wait_recv()
        for a in range(2):
            wmat = (wa[:, :, gg] if a == 0 else wb[gg]).reshape(NY * 2 * 32, H * HD)
            total_out[a] += dot_nt(ab[gg], wmat)
    for a in range(2):
        out_ref[:, a * 512:(a + 1) * 512] = total_out[a].astype(jnp.bfloat16)

    @pl.when(zh == 0)
    def _():
        zsend.wait_send()

    @pl.when(zh == 1)
    def _():
        for s in far1 + far2:
            s.wait_send()
        far_half.wait_send()

    for s in near1 + near2 + qsend + [near_half] + wx + wy1 + wy2 + cross1 + cross2 + ox + sx + ax:
        s.wait_send()
    first_hop(0, 1).wait_send()

    @pl.when(jnp.logical_not(own_w))
    def _():
        first_hop(0, 0).wait_send()

    for sign, step, p in all_ring:
        ring(sign, step, p).wait_send()
    for i in range(NY):
        w_over(yp(i), i).wait_send()
    for d in range(NX):
        wb_over(d).wait_send()


def body(queries, keys, values, lengths, out_weight):
    steps = np.arange(HD // 2) * (2.0 / HD)
    inverse = (500000.0 ** -steps).astype(np.float32)
    inverse = jnp.asarray(np.concatenate([inverse, inverse])[None, :])
    vmem = pl.BlockSpec(memory_space=pltpu.VMEM)
    dma = pltpu.SemaphoreType.DMA
    bf, f32 = jnp.bfloat16, jnp.float32
    return pl.pallas_call(
        kernel,
        out_shape=(jax.ShapeDtypeStruct((T, 1024), bf), jax.ShapeDtypeStruct((T, HD), bf)),
        in_specs=[vmem] * 6,
        out_specs=(vmem, vmem),
        scratch_shapes=[
            pltpu.VMEM((2, 2, NY, 2, T, HD), bf),
            pltpu.VMEM((NX, R, HD), bf),
            pltpu.VMEM((NX, R, HD), f32),
            pltpu.VMEM((NX, R, HD), f32),
            pltpu.VMEM((NX, R, HD), f32),
            pltpu.VMEM((NX, R, HD), bf),
            pltpu.VMEM((NX, 8, R), f32),
            pltpu.VMEM((NX, R, HD), bf),
            pltpu.VMEM((NX, 8, R), f32),
            pltpu.VMEM((G, T, H * HD), bf),
            pltpu.VMEM((NY, 2, G, 32, H * HD), bf),
            pltpu.VMEM((G, NY, 2, 32, H * HD), bf),
            pltpu.VMEM((NX, R, HD), f32),
            dma((8,)), dma((8,)),
            dma, dma,
            dma((8,)), dma((8,)),
            dma((2,)), dma((2,)),
            dma((NX - 1,)), dma((NX - 1,)),
            dma((NX - 1,)), dma((NX - 1,)),
            dma((NX - 1,)), dma((NX - 1,)),
            dma((G - 1,)), dma((G - 1,)),
            dma((2,)), dma((2,)),
            dma((NX - 1,)), dma((NX - 1,)),
            dma((8,)), dma((8,)),
            dma((4,)), dma((4,)),
            dma((2, 4, 2)), dma((2, 4, 2)),
            dma((NY,)), dma((NY,)),
            dma((NX,)), dma((NX,)),
            dma,
        ],
        compiler_params=pltpu.CompilerParams(
            collective_id=0, has_side_effects=True, vmem_limit_bytes=56 * 2**20
        ),
    )(queries, keys, values, lengths.reshape(1, 64), out_weight, inverse)


def solution(mesh):
    return jax.shard_map(
        body,
        mesh=mesh,
        in_specs=(P("blk", "kv"), P("blk", "kv"), P("blk", "kv"), P(), P("blk", "kv")),
        out_specs=(P("blk", "kv"), P("blk", "kv")),
        check_vma=False,
    )
```

```python
import functools

import jax
import jax.numpy as jnp
import numpy as np
from jax import lax
from jax.experimental import pallas as pl
from jax.experimental.pallas import tpu as pltpu
from jax.sharding import PartitionSpec as P

MESH = pl.DeviceIdType.MESH
T, HD, H, NX, NY, G = 80, 128, 4, 4, 8, 4
R = H * T
SUP = 16 * T
CH = NY * T
LONG_BLOCKS = 102
LONG_TOKENS = 8192
TOKENS = 10240
NEG = -1e30
PLAN = ("WFT", "R", "Xa", "", "1", "", "2", "b3", "E4")
SCALE = float(np.log2(np.e) / np.sqrt(HD))


def dot_nt(a, b):
    return lax.dot_general(a, b, (((1,), (1,)), ((), ())), preferred_element_type=jnp.float32)


def kernel(
    q_ref, k_ref, v_ref, len_ref, w_ref, inv_ref, out_ref, cache_ref,
    kv, qb, acc, mx, sm, osend, ssend, obuf, sbuf, ab, wa, wb, col,
    ys, yr, zs, zr, fs, fr, cs, cr, qs, qr, os_, or_, ss, sr, as_, ar, wds, wdr, wxs, wxr, wys, wyr, wbs, wbr, wrs, wrr, wcs, wcr, wes, wer, lsem,
):
    blk, g = lax.axis_index("blk"), lax.axis_index("kv")
    c = lax.rem(blk, 2)
    y = lax.rem(lax.div(blk, 2), NY)
    x = lax.rem(lax.div(blk, 16), NX)
    zh = lax.div(blk, 64)
    dest_g = 2 * zh + lax.div(x, 2)
    half = lax.rem(x, 2)

    def at(zh_=zh, x_=x, y_=y, c_=c, g_=g):
        return {"blk": ((zh_ * NX + x_) * NY + y_) * 2 + c_, "kv": g_}

    def send(src, dst, s, r, dev):
        return pltpu.make_async_remote_copy(
            src_ref=src, dst_ref=dst, send_sem=s, recv_sem=r, device_id=dev, device_id_type=MESH
        )

    def yp(d):
        return lax.rem(y + d + NY, NY)

    def xp(d):
        return lax.rem(x + d, NX)

    def gp(d):
        return lax.rem(g + d, G)

    bar = pltpu.get_barrier_semaphore()

    def hello(dev):
        pl.semaphore_signal(bar, inc=1, device_id=dev, device_id_type=MESH)

    hello(at(zh_=1 - zh))
    hello(at(c_=1 - c))
    for d in range(1, NY):
        hello(at(y_=yp(d)))
    for d in range(1, NX):
        hello(at(x_=xp(d)))
    for d in range(1, G):
        hello(at(g_=gp(d)))
    src_zh, src_x = lax.div(g, 2), 2 * lax.rem(g, 2)
    own_w = (x == g) & (dest_g == g)
    for a in range(2):
        @pl.when(jnp.logical_not(own_w & (half == a)))
        def _(a=a):
            hello(at(zh_=src_zh, x_=src_x + a, g_=x))

    lens = jnp.broadcast_to(len_ref[...].astype(jnp.float32), (8, 64))
    tri = (lax.broadcasted_iota(jnp.int32, (64, 64), 0) < lax.broadcasted_iota(jnp.int32, (64, 64), 1))
    before = jnp.dot(lens, tri.astype(jnp.float32), preferred_element_type=jnp.float32)[:1]
    starts = before + (TOKENS - jnp.sum(lens[:1], axis=1, keepdims=True))

    def first_of(tok):
        return jnp.max(jnp.where(starts <= tok, starts, 0.0), axis=1, keepdims=True)

    row = lax.broadcasted_iota(jnp.int32, (T, 1), 0)
    tok = (row + blk * T).astype(jnp.float32)
    angle = (tok - first_of(tok)) * inv_ref[...]
    cosine = jnp.cos(angle)
    lane = lax.broadcasted_iota(jnp.int32, (T, HD), 1)
    sine = jnp.where(lane < HD // 2, -1.0, 1.0) * jnp.sin(angle)

    def rotate(f):
        f = f.astype(jnp.float32)
        return (f * cosine + pltpu.roll(f, HD // 2, 1) * sine).astype(jnp.bfloat16)

    rk = rotate(k_ref[...])
    cache_ref[...] = rk
    kv[zh, c, y, 0] = rk
    kv[zh, c, y, 1] = v_ref[...]
    for h in range(H):
        qb[x, h * T:(h + 1) * T, :] = rotate(q_ref[:, h * HD:(h + 1) * HD])

    pl.semaphore_wait(bar, 2 + (NY - 1) + (NX - 1) + (G - 1) + 2 - jnp.where(own_w, 1, 0))

    mine = kv.at[zh, c, y]
    zsend = send(mine, mine, zs, zr, at(zh_=1 - zh))

    @pl.when(zh == 0)
    def _():
        zsend.start()

    def tree(zk, ss_, rs_):
        me = kv.at[zk, c, y]
        first = [send(me, me, ss_.at[i], rs_.at[i], at(y_=yp(d))) for i, d in enumerate((2, -2, 1, -1))]
        second = []
        for i, sign in enumerate((1, -1)):
            whole = kv.at[zk, c, yp(-2 * sign)]
            part = kv.at[zk, c, yp(-2 * sign), i]
            second.append(send(whole, whole, ss_.at[4 + i], rs_.at[4 + i], at(y_=yp(sign))))
            second.append(send(part, part, ss_.at[6 + i], rs_.at[6 + i], at(y_=yp(2 * sign))))
        return first, second

    near1, near2 = tree(zh, ys, yr)
    far1, far2 = tree(0, fs, fr)
    qsend = [send(qb.at[x], qb.at[x], qs.at[d - 1], qr.at[d - 1], at(x_=xp(d))) for d in range(1, NX)]

    def first_hop(a, dz):
        slot = wa.at[y, c, g] if a == 0 else wb.at[g, y, c]
        return send(w_ref, slot, wds.at[dz], wdr.at[a], at(zh_=lax.rem(zh + dz, 2), x_=g, g_=dest_g))

    def own_copy(a):
        return pltpu.make_async_copy(w_ref, wa.at[y, c, g] if a == 0 else wb.at[g, y, c], lsem)

    for a in range(2):
        @pl.when(half == a)
        def _(a=a):
            first_hop(a, 1).start()

            @pl.when(own_w)
            def _():
                own_copy(a).start()

            @pl.when(jnp.logical_not(own_w))
            def _():
                first_hop(a, 0).start()

    for s in near1 + qsend:
        s.start()

    for i in range(NX):
        tk = (row + ((zh * NX + i) * 16 + 2 * y + c) * T).astype(jnp.float32)
        st = first_of(tk)
        both = jnp.where(lax.broadcasted_iota(jnp.int32, (T, HD), 1) == 0, tk, st)
        for h in range(H):
            col[i, h * T:(h + 1) * T, :] = both
    mx[...] = jnp.full(mx.shape, NEG, jnp.float32)
    sm[...] = jnp.zeros(sm.shape, jnp.float32)
    acc[...] = jnp.zeros(acc.shape, jnp.float32)

    def second(first, then):
        for s in first[:2]:
            s.wait_recv()
        for s in then:
            s.start()

    second(near1, near2)

    @pl.when(zh == 1)
    def _():
        zsend.wait_recv()
        for s in far1:
            s.start()

    def far_second():
        @pl.when(zh == 1)
        def _():
            second(far1, far2)

    whole_y = wb.at[x, y, c]
    wy1 = [send(whole_y, whole_y, wys.at[i], wyr.at[i], at(y_=yp(d))) for i, d in enumerate((2, -2, 1, -1))]
    wy2 = []
    for i, sign in enumerate((1, -1)):
        full = wb.at[x, yp(-2 * sign), c]
        part = wb.at[x, yp(-2 * sign), c, pl.ds(16 * i, 16)]
        wy2.append(send(full, full, wys.at[4 + i], wyr.at[4 + i], at(y_=yp(sign))))
        wy2.append(send(part, part, wys.at[6 + i], wyr.at[6 + i], at(y_=yp(2 * sign))))
    wx = [send(wa.at[y, c, x], wa.at[y, c, x], wxs.at[d - 1], wxr.at[d - 1], at(x_=xp(d))) for d in range(1, NX)]

    whole_x = wb.at[x, :, c]
    cross1 = [send(whole_x, whole_x, wbs.at[i], wbr.at[i], at(x_=xp(d))) for i, d in enumerate((1, NX - 1))]
    cross2 = []
    for i, d in enumerate((1, NX - 1)):
        part = wb.at[xp(NX - d), pl.ds(4 * i, 4), c]
        cross2.append(send(part, part, wbs.at[2 + i], wbr.at[2 + i], at(x_=xp(d))))

    def ring(sign, step, p):
        i = 0 if sign > 0 else 1
        piece = wa.at[yp(-sign * (step - 1)), c, pl.ds(2 * p, 2)]
        return send(piece, piece, wrs.at[i, step - 1, p], wrr.at[i, step - 1, p], at(y_=yp(sign)))

    def ring_pieces(sign, step):
        return (0, 1) if step < 4 else ((0,) if sign > 0 else (1,))

    def w_over(yy, i):
        return send(wa.at[yy, c], wa.at[yy, c], wcs.at[i], wcr.at[i], at(c_=1 - c))

    def wb_over(d):
        part = wb.at[xp(d), :, c]
        return send(part, part, wes.at[d], wer.at[d], at(c_=1 - c))

    all_ring = [(sign, step, p) for step in range(1, 5) for sign in (1, -1) for p in ring_pieces(sign, step)]

    def w_first():
        for a in range(2):
            here = own_w & (half == a)

            @pl.when(here)
            def _(a=a):
                own_copy(a).wait()

            @pl.when(jnp.logical_not(here))
            def _(a=a):
                first_hop(a, 0).wait_recv()
        for s in wx:
            s.start()
        for s in wy1:
            s.start()

    def w_ring_begin():
        for s in wx:
            s.wait_recv()
        for p in range(2):
            for sign in (1, -1):
                ring(sign, 1, p).start()
        w_over(y, 0).start()

    def chunk(zk, ck):
        sk = zk * NX + x
        r = lax.broadcasted_iota(jnp.int32, (1, CH), 1)
        key_tok = ((r + lax.div(r, T) * T) + sk * SUP + ck * T).astype(jnp.float32)

        def one(i, _):
            sq = zh * NX + i
            b = sq * 16 + 2 * y + c
            near = (sk == sq) | ((sk == sq - 1) & (2 * y + c == 0))
            live = (sk <= sq) & ((b <= LONG_BLOCKS) | near)
            edge = (sk == sq) | (b >= LONG_BLOCKS)

            def work(masked):
                keys = kv[zk, ck, :, 0].reshape(CH, HD)
                vals = kv[zk, ck, :, 1].reshape(CH, HD)
                s = dot_nt(qb[i], keys) * SCALE
                if masked:
                    ok = (key_tok <= col[i, :, 0:1]) & (key_tok >= col[i, :, 1:2])
                    s = jnp.where(ok, s, NEG)
                old = mx[i, :, 0:1]
                new = jnp.maximum(old, jnp.max(s, axis=1, keepdims=True))
                p = jnp.exp2(s - new)
                if masked:
                    p = jnp.where(ok, p, 0.0)
                keep = jnp.exp2(old - new)
                sm[i] = jnp.broadcast_to(sm[i, :, 0:1] * keep + jnp.sum(p, axis=1, keepdims=True), (R, HD))
                mx[i] = jnp.broadcast_to(new, (R, HD))
                acc[i] = acc[i] * keep + jnp.dot(p.astype(jnp.bfloat16), vals, preferred_element_type=jnp.float32)

            @pl.when(live & edge)
            def _():
                work(True)

            @pl.when(live & jnp.logical_not(edge))
            def _():
                work(False)

            return 0

        lax.fori_loop(0, NX, one, 0)

    def over(zk, i):
        return send(kv.at[zk, c], kv.at[zk, c], cs.at[i], cr.at[i], at(c_=1 - c))

    def w_cross():
        for s in wy1[2:] + wy2:
            s.wait_recv()
        wb_over(0).start()

    def w_cross_one():
        for s in cross1:
            s.start()

    def w_cross_two():
        for s in cross1:
            s.wait_recv()
        for s in cross2:
            s.start()
        wb_over(1).start()
        wb_over(NX - 1).start()

    def w_cross_end():
        for s in cross2:
            s.wait_recv()
        wb_over(2).start()

    def w_step(step):
        for p in range(2):
            for sign in (1, -1):
                if p in ring_pieces(sign, step):
                    ring(sign, step, p).wait_recv()
                    if step < 4 and p in ring_pieces(sign, step + 1):
                        ring(sign, step + 1, p).start()
        w_over(yp(step), step).start()
        if step < 4:
            w_over(yp(-step), 8 - step).start()

    work = {
        "W": w_first, "R": w_ring_begin, "X": w_cross, "E": w_cross_end,
        "a": w_cross_one, "b": w_cross_two, "F": far_second, "T": lambda: second(wy1, wy2),
    }
    for step in range(1, 5):
        work[str(step)] = functools.partial(w_step, step)

    def turn(i):
        for name in PLAN[i]:
            work[name]()

    near_half = over(zh, 0)
    far_half = over(0, 1)
    turn(0)
    for s in near1[2:] + near2:
        s.wait_recv()
    near_half.start()
    for s in qsend:
        s.wait_recv()
    turn(1)

    def stage(i, _):
        @pl.when(i == 1)
        def _():
            turn(2)
            near_half.wait_recv()

        @pl.when(i == 2)
        def _():
            turn(3)

            @pl.when(zh == 1)
            def _():
                for s in far1[2:] + far2:
                    s.wait_recv()
                far_half.start()

            turn(4)

        @pl.when(i == 3)
        def _():
            turn(5)

            @pl.when(zh == 1)
            def _():
                far_half.wait_recv()

        @pl.when((i < 2) | (zh == 1))
        def _():
            chunk(jnp.where(i < 2, zh, 0), jnp.where(lax.rem(i, 2) == 0, c, 1 - c))

        return 0

    lax.fori_loop(0, 4, stage, 0)
    turn(6)

    lane_r = lax.broadcasted_iota(jnp.int32, (R, HD), 1)

    def pack(i):
        osend[i] = acc[i].astype(jnp.bfloat16)
        ssend[i] = jnp.transpose(jnp.where(lane_r == 0, mx[i], sm[i]))[:8]

    ox = [send(osend.at[xp(d)], obuf.at[x], os_.at[d - 1], or_.at[d - 1], at(x_=xp(d))) for d in range(1, NX)]
    sx = [send(ssend.at[xp(d)], sbuf.at[x], ss.at[d - 1], sr.at[d - 1], at(x_=xp(d))) for d in range(1, NX)]
    for d in (2, 1, 3, 0):
        pack(xp(d))
        if d:
            ox[d - 1].start()
            sx[d - 1].start()
    turn(7)
    for s in sx + ox:
        s.wait_recv()
    stats = [ssend[x]] + [sbuf[xp(d)] for d in range(1, NX)]
    parts = [osend[x]] + [obuf[xp(d)] for d in range(1, NX)]
    top = functools.reduce(jnp.maximum, [s[0:1] for s in stats])
    weight = [jnp.exp2(s[0:1] - top) for s in stats]
    total = sum(s[1:2] * w for s, w in zip(stats, weight))
    att = 0.0
    for o, w in zip(parts, weight):
        att += o.astype(jnp.float32) * jnp.transpose(jnp.broadcast_to(w / total, (HD, R)))
    for h in range(H):
        ab[g, :, h * HD:(h + 1) * HD] = att[h * T:(h + 1) * T].astype(jnp.bfloat16)

    ax = [send(ab.at[g], ab.at[g], as_.at[d - 1], ar.at[d - 1], at(g_=gp(d))) for d in range(1, G)]
    for s in ax:
        s.start()
    turn(8)
    for i in range(NY):
        w_over(yp(i), i).wait_recv()
    for d in range(NX):
        wb_over(d).wait_recv()

    total_out = [0.0, 0.0]
    for d in range(G):
        gg = gp(d)
        if d:
            ax[G - d - 1].wait_recv()
        for a in range(2):
            wmat = (wa[:, :, gg] if a == 0 else wb[gg]).reshape(NY * 2 * 32, H * HD)
            total_out[a] += dot_nt(ab[gg], wmat)
    for a in range(2):
        out_ref[:, a * 512:(a + 1) * 512] = total_out[a].astype(jnp.bfloat16)

    @pl.when(zh == 0)
    def _():
        zsend.wait_send()

    @pl.when(zh == 1)
    def _():
        for s in far1 + far2:
            s.wait_send()
        far_half.wait_send()

    for s in near1 + near2 + qsend + [near_half] + wx + wy1 + wy2 + cross1 + cross2 + ox + sx + ax:
        s.wait_send()
    first_hop(0, 1).wait_send()

    @pl.when(jnp.logical_not(own_w))
    def _():
        first_hop(0, 0).wait_send()

    for sign, step, p in all_ring:
        ring(sign, step, p).wait_send()
    for i in range(NY):
        w_over(yp(i), i).wait_send()
    for d in range(NX):
        wb_over(d).wait_send()


def body(queries, keys, values, lengths, out_weight):
    steps = np.arange(HD // 2) * (2.0 / HD)
    inverse = (500000.0 ** -steps).astype(np.float32)
    inverse = jnp.asarray(np.concatenate([inverse, inverse])[None, :])
    vmem = pl.BlockSpec(memory_space=pltpu.VMEM)
    dma = pltpu.SemaphoreType.DMA
    bf, f32 = jnp.bfloat16, jnp.float32
    return pl.pallas_call(
        kernel,
        out_shape=(jax.ShapeDtypeStruct((T, 1024), bf), jax.ShapeDtypeStruct((T, HD), bf)),
        in_specs=[vmem] * 6,
        out_specs=(vmem, vmem),
        scratch_shapes=[
            pltpu.VMEM((2, 2, NY, 2, T, HD), bf),
            pltpu.VMEM((NX, R, HD), bf),
            pltpu.VMEM((NX, R, HD), f32),
            pltpu.VMEM((NX, R, HD), f32),
            pltpu.VMEM((NX, R, HD), f32),
            pltpu.VMEM((NX, R, HD), bf),
            pltpu.VMEM((NX, 8, R), f32),
            pltpu.VMEM((NX, R, HD), bf),
            pltpu.VMEM((NX, 8, R), f32),
            pltpu.VMEM((G, T, H * HD), bf),
            pltpu.VMEM((NY, 2, G, 32, H * HD), bf),
            pltpu.VMEM((G, NY, 2, 32, H * HD), bf),
            pltpu.VMEM((NX, R, HD), f32),
            dma((8,)), dma((8,)),
            dma, dma,
            dma((8,)), dma((8,)),
            dma((2,)), dma((2,)),
            dma((NX - 1,)), dma((NX - 1,)),
            dma((NX - 1,)), dma((NX - 1,)),
            dma((NX - 1,)), dma((NX - 1,)),
            dma((G - 1,)), dma((G - 1,)),
            dma((2,)), dma((2,)),
            dma((NX - 1,)), dma((NX - 1,)),
            dma((8,)), dma((8,)),
            dma((4,)), dma((4,)),
            dma((2, 4, 2)), dma((2, 4, 2)),
            dma((NY,)), dma((NY,)),
            dma((NX,)), dma((NX,)),
            dma,
        ],
        compiler_params=pltpu.CompilerParams(
            collective_id=0, has_side_effects=True, vmem_limit_bytes=56 * 2**20
        ),
    )(queries, keys, values, lengths.reshape(1, 64), out_weight, inverse)


def solution(mesh):
    return jax.shard_map(
        body,
        mesh=mesh,
        in_specs=(P("blk", "kv"), P("blk", "kv"), P("blk", "kv"), P(), P("blk", "kv")),
        out_specs=(P("blk", "kv"), P("blk", "kv")),
        check_vma=False,
    )
```
